256 devices in a mesh: gx: 4 (over z_lo), gy: 8 (over y, z_hi), gz: 8 (over x, core).
Axes of the slice: x: 4, y: 4, z: 8 (z_hi: 2, z_lo: 4; z = z_hi * 4 + z_lo), core: 2. Of those that a mesh axis runs over, the one named last changes fastest.
Arguments:
- inputs: float32 [2048, 4096], P('gz', 'gx'), may hold values from -6 to 6
- pre_act: float32 [2048, 8192], P('gz', 'gy'), may hold values from -6 to 6
- w_in: float32 [4096, 8192], P('gx', 'gy'), may hold values from -0.75 to 0.75
- w_out: float32 [8192, 4096], P('gy', 'gx'), may hold values from -0.0625 to 0.0625
- grad_out: float32 [2048, 4096], P('gz', 'gx'), may hold values from -0.6 to 0.6
Outputs:
- grad_inputs: float32 [2048, 4096], P('gz', ('gx', 'gy'))
- grad_w_in: float32 [4096, 8192], P('gx', ('gy', 'gz'))
- grad_w_out: float32 [8192, 4096], P(('gy', 'gz'), 'gx')
The draws below stay inside these ranges and needn't reach their ends.
All inputs are finite; a program needn't handle non-finite values.
Results may differ from the reference program's by a relative error of at most 0.000096.
Values sent between devices are 32-bit elements; how exact they have to be, the bound alone decides.
A program may use at most 128 MiB of HBM per device.

```python
import jax
import jax.numpy as jnp
from jax import lax

D = 4096
FF = 8192
TOKENS = 2048


def levels(own_key, dims, pieces, low, largest):
    def one(axis_at, shards_of):
        steps = jax.random.uniform(jax.random.fold_in(jax.random.fold_in(own_key, 6), axis_at), (shards_of,), jnp.float32, low / len(pieces), largest / len(pieces))
        return jnp.repeat(jnp.exp(steps), dims[axis_at] // shards_of).reshape((-1,) + (1,) * (len(dims) - axis_at - 1))

    level = one(*pieces[0])
    for cut in pieces[1:]:
        level = level * one(*cut)
    return level


def gaussian(stream_key, dims, scale, bound, split=(), dtype=jnp.bfloat16):
    drawn = jax.random.normal(stream_key, dims, jnp.float32) * scale
    if len(split) > 0:
        drawn = levels(stream_key, dims, split, -0.22, 0.18) * drawn
    return jnp.clip(drawn, min=-bound, max=bound).astype(dtype)


def setup_inputs(seed: int = 0) -> dict:
    seeds = jax.random.split(jax.random.key(seed), 6)
    return {
        "inputs": gaussian(seeds[0], (TOKENS, D), 1.0, 6.0, ((0, 8), (1, 4)), jnp.float32),
        "pre_act": gaussian(seeds[1], (TOKENS, FF), 1.0, 6.0, ((0, 8), (1, 8)), jnp.float32),
        "w_in": gaussian(seeds[2], (D, FF), (D // 64) ** -0.5, 0.75, ((0, 4), (1, 8)), jnp.float32),
        "w_out": gaussian(seeds[3], (FF, D), FF ** -0.5, 0.0625, ((0, 8), (1, 4)), jnp.float32),
        "grad_out": gaussian(seeds[4], (TOKENS, D), 0.1, 0.6, ((0, 8), (1, 4)), jnp.float32),
    }


sqrt_two_pi = 0.7978845608028654
cubic_coef = 0.044715

def gelu_parts(values):
    inner = sqrt_two_pi * (values + cubic_coef * values * values * values)
    tangent = jnp.tanh(inner)
    activation = 0.5 * values * (1.0 + tangent)
    derivative = 0.5 * (1.0 + tangent) + 0.5 * values * (1.0 - tangent * tangent) * sqrt_two_pi * (1.0 + 3.0 * cubic_coef * values * values)
    return (activation, derivative)

def matmul(left, right):
    return jnp.dot(left, right, preferred_element_type=jnp.float32, precision=lax.Precision.HIGHEST)

def reference(inputs, pre_act, w_in, w_out, grad_out):
    activation, derivative = gelu_parts(pre_act)
    grad_act = matmul(grad_out, w_out.T)
    grad_hidden = grad_act * derivative
    grad_inputs = matmul(grad_hidden, w_in.T)
    grad_w_in = matmul(inputs.T, grad_hidden)
    grad_w_out = matmul(activation.T, grad_out)
    return (grad_inputs, grad_w_in, grad_w_out)
```

```python
import functools

import jax
import jax.numpy as jnp
from jax import lax
from jax.experimental import pallas as pl
from jax.experimental.pallas import tpu as pltpu
from jax.sharding import PartitionSpec as P

MESH = pl.DeviceIdType.MESH
F32 = jnp.float32
BF16 = jnp.bfloat16
sqrt_two_pi = 0.7978845608028654
cubic_coef = 0.044715

TOK = 256
WID = 1024
BLK = 128
HALF = 512
PARTS = 2
ROWS = TOK // PARTS
CHUNKS = [(k, e, t) for t in range(PARTS) for k in range(4) for e in range(2)]
LAG = 2
FLIGHT = 3

NN = (((1,), (0,)), ((), ()))
NT = (((1,), (1,)), ((), ()))


def split(value):
    high = value.astype(BF16)
    return high, (value - high.astype(F32)).astype(BF16)


def dot3(left, right, dims):
    (lh, ll), (rh, rl) = left, right
    d = lambda a, b: lax.dot_general(a, b, dims, preferred_element_type=F32)
    return d(lh, rh) + (d(lh, rl) + d(ll, rh))


def tangent_of(v):
    return jnp.tanh(sqrt_two_pi * (v + cubic_coef * v * v * v))


def gelu_value(v, t):
    return 0.5 * v * (1.0 + t)


def gelu_slope(v, t):
    return 0.5 * (1.0 + t) + 0.5 * v * (1.0 - t * t) * sqrt_two_pi * (1.0 + 3.0 * cubic_coef * v * v)


def kernel(
    x_in, p_in, wi_in, wo_in, g_in, gi_out, gwi_out, gwo_out,
    g_v, gs_v, g_h, g_l, wo_v, wo_h, wo_l, wi_v, wi_h, wi_l, x_v, xs_v, x_h, x_l,
    p_v, ps_v, der_v, a_h, a_l, h_h, h_l, own_z, rp, rs, sp, ss, hid_h, hid_l, hsend, hs_v,
    xsend, xrecv, xown, ysend, yrecv, yown, hsnd, hrcv, gi_v, gwi_v, gwo_v,
    lsem, osem, csend, crecv, zsend, zrecv, xss, xrs, yss, yrs, vss, vrs,
):
    gx, gy, gz = lax.axis_index("gx"), lax.axis_index("gy"), lax.axis_index("gz")
    y, zh, x, c = gy // 2, gy % 2, gz // 2, gz % 2
    xp, xm, xo = (x + 1) % 4, (x + 3) % 4, (x + 2) % 4
    yp, ym, yo = (y + 1) % 4, (y + 3) % 4, (y + 2) % 4
    owners = (xo, xp, xm, x)
    yowners = (yo, yp, ym, y)
    sibling = (gx, gy, x * 2 + 1 - c)
    x_next, x_prev = (gx, gy, xp * 2 + c), (gx, gy, xm * 2 + c)
    y_next, y_prev = (gx, yp * 2 + zh, gz), (gx, ym * 2 + zh, gz)
    partner = (gx, y * 2 + 1 - zh, gz)
    zr, zl = (gx + 1) % 4, (gx + 3) % 4
    z_next = (zr, y * 2 + jnp.where(gx == 3, 1 - zh, zh), gz)
    z_prev = (zl, y * 2 + jnp.where(gx == 0, 1 - zh, zh), gz)

    def block(k, e):
        return 2 * owners[k] + (c if e else 1 - c)

    def cols(k, e):
        return pl.ds(pl.multiple_of(block(k, e) * BLK, BLK), BLK)

    def load(src, dst, n):
        return pltpu.make_async_copy(src, dst, lsem.at[n])

    l_g = load(g_in, g_v, 0)
    l_wo = [[load(wo_in.at[cols(k, e), :], wo_v.at[2 * k + e], 1 + 2 * k + e) for e in range(2)] for k in range(4)]
    l_p = [[load(p_in.at[:, cols(k, e)], p_v.at[2 * k + e], 9 + 2 * k + e) for e in range(2)] for k in range(4)]
    l_x = load(x_in, x_v, 17)
    l_wi = [
        load(wi_in.at[pl.ds(pl.multiple_of(yowners[n] * TOK, TOK), TOK), :], wi_v.at[n], 18 + n) for n in range(4)
    ]
    l_g.start()
    for k in range(4):
        for e in range(2):
            l_wo[k][e].start()
        if k == 0:
            for j in range(4):
                for e in range(2):
                    l_p[j][e].start()
    l_x.start()
    for n in range(4):
        l_wi[n].start()

    barrier = pltpu.get_barrier_semaphore()
    for who in (sibling, x_next, x_prev, y_next, y_prev, z_next, z_prev, partner):
        pl.semaphore_signal(barrier, inc=1, device_id=who, device_id_type=MESH)
    pl.semaphore_wait(barrier, 8)

    def remote(src, dst, s_sem, r_sem, who):
        return pltpu.make_async_remote_copy(
            src_ref=src, dst_ref=dst, send_sem=s_sem, recv_sem=r_sem, device_id=who, device_id_type=MESH
        )

    c_p = [remote(p_in.at[:, cols(k, 0)], ps_v.at[k], csend.at[k], crecv.at[k], sibling) for k in range(4)]
    c_g = [
        remote(g_in.at[:, pl.ds(h * HALF, HALF)], gs_v.at[h], csend.at[4 + h], crecv.at[4 + h], sibling)
        for h in range(2)
    ]
    c_x = remote(x_in, xs_v, csend.at[6], crecv.at[6], sibling)
    c_h = [remote(hsend.at[k], hs_v.at[k], csend.at[7 + k], crecv.at[7 + k], sibling) for k in range(4)]
    c_p[0].start()
    c_g[0].start()
    c_g[1].start()
    for k in range(1, 4):
        c_p[k].start()
    c_x.start()

    @pl.when(gx == 0)
    def _():
        rp[...] = jnp.zeros_like(rp)

    @pl.when(gx == 3)
    def _():
        rs[...] = jnp.zeros_like(rs)

    def where(i):
        k, e, t = CHUNKS[i]
        return (2 * k + e, pl.ds(t * ROWS, ROWS))

    def z_copy(src, dst, way, i):
        b, rows = where(i)
        return remote(
            src.at[b, rows], dst.at[b, rows], zsend.at[way, i], zrecv.at[way, i], z_next if way == 0 else z_prev
        )

    def right(i, src=None):
        return z_copy(sp if src is None else src, rp, 0, i)

    def left(i, src=None):
        return z_copy(ss if src is None else src, rs, 1, i)

    def z_own(i):
        @pl.when(gx == 0)
        def _():
            if i >= FLIGHT:
                right(i - FLIGHT).wait_send()
            right(i, own_z).start()

        @pl.when(gx == 3)
        def _():
            if i >= FLIGHT:
                left(i - FLIGHT).wait_send()
            left(i, own_z).start()

    def forward_right(i):
        b, rows = where(i)
        right(i).wait_recv()
        sp[b, rows] = own_z[b, rows] + rp[b, rows]
        right(i).start()

    def forward_left(i):
        b, rows = where(i)
        left(i).wait_recv()
        ss[b, rows] = own_z[b, rows] + rs[b, rows]
        left(i).start()

    def z_near(i):
        pl.when(gx == 1)(lambda: forward_right(i))
        pl.when(gx == 2)(lambda: forward_left(i))

    def z_far(i):
        pl.when(gx == 1)(lambda: forward_left(i))
        pl.when(gx == 2)(lambda: forward_right(i))

    def z_final(i):
        k, e, t = CHUNKS[i]
        b, rows = where(i)

        @pl.when(gx == 0)
        def _():
            left(i).wait_recv()

        @pl.when(gx == 3)
        def _():
            right(i).wait_recv()

        hidden = (own_z[b, rows] + rp[b, rows] + rs[b, rows]) * der_v[b, rows]
        high, low = split(hidden)
        hid_h[rows, cols(k, e)] = high
        hid_l[rows, cols(k, e)] = low
        if e == 0:
            hsend[k, rows] = hidden
            if t == PARTS - 1:
                c_h[k].start()
        else:
            high, low = split(hidden.T)
            h_h[k, :, rows] = high
            h_l[k, :, rows] = low

    def z_step(i):
        n = len(CHUNKS)
        if 0 <= i < n:
            z_own(i)
        if 0 <= i - 1 < n:
            z_near(i - 1)
        if 0 <= i - 1 - LAG < n:
            z_far(i - 1 - LAG)
        if 0 <= i - 1 - 2 * LAG < n:
            z_final(i - 1 - 2 * LAG)

    def partial(k):
        for e in range(2):
            l_wo[k][e].wait()
            b = 2 * k + e
            wo_h[pl.ds(b * BLK, BLK), :], wo_l[pl.ds(b * BLK, BLK), :] = split(wo_v[b])
        rows = pl.ds(2 * k * BLK, 2 * BLK)
        value = dot3((g_h[:TOK, :], g_l[:TOK, :]), (wo_h[rows, :], wo_l[rows, :]), NT)
        own_z[2 * k] = value[:, :BLK]
        own_z[2 * k + 1] = value[:, BLK:]

    def gelu(k):
        for e in range(2):
            l_p[k][e].wait()
            v = p_v[2 * k + e]
            t = tangent_of(v)
            der_v[2 * k + e] = gelu_slope(v, t)
            if e == 1:
                a_h[k, :, :TOK], a_l[k, :, :TOK] = split(gelu_value(v, t).T)
        c_p[k].wait_recv()
        v = ps_v[k]
        a_h[k, :, TOK:], a_l[k, :, TOK:] = split(gelu_value(v, tangent_of(v)).T)

    def x_copy(g, m):
        return remote(xsend.at[g, m], xrecv.at[g, m], xss.at[g, m], xrs.at[g, m], x_next if m % 2 == 0 else x_prev)

    def weight(g, k, h):
        th, tl, vh, vl = (a_h, a_l, g_h, g_l) if g == 0 else (h_h, h_l, x_h, x_l)
        half = pl.ds(h * HALF, HALF)
        return dot3((th[k], tl[k]), (vh[:, half], vl[:, half]), NN)

    def x_send(g, m, k, h):
        xsend[g, m] = weight(g, k, h)
        x_copy(g, m).start()

    def x_first(g):
        x_send(g, 1, 0, 0)
        x_send(g, 0, 0, 1)

    def x_second(g):
        x_send(g, 2, 1, 0)
        x_send(g, 3, 2, 1)

    def x_third_local(g):
        xsend[g, 4] = weight(g, 1, 1)
        xsend[g, 5] = weight(g, 2, 0)

    def x_third(g):
        for m in (4, 5):
            x_copy(g, m - 4).wait_recv()
            xsend[g, m] = xsend[g, m] + xrecv[g, m - 4]
            x_copy(g, m).start()

    def x_own(g):
        xown[g, 0] = weight(g, 3, 0)
        xown[g, 1] = weight(g, 3, 1)

    def x_final(g):
        for h, ms in ((0, (2, 5)), (1, (3, 4))):
            for m in ms:
                x_copy(g, m).wait_recv()
            total = xown[g, h] + xrecv[g, ms[0]] + xrecv[g, ms[1]]
            half = pl.ds(h * HALF, HALF)
            if g == 0:
                gwo_v[:, half] = total
            else:
                gwi_v[half, :] = total.T
        if g == 0:
            pltpu.make_async_copy(gwo_v, gwo_out, osem.at[0]).start()
        else:
            pltpu.make_async_copy(gwi_v, gwi_out, osem.at[1]).start()

    def hidden_sibling(k):
        c_h[k].wait_recv()
        h_h[k, :, TOK:], h_l[k, :, TOK:] = split(hs_v[k].T)

    def split_inputs():
        l_x.wait()
        x_h[:TOK, :], x_l[:TOK, :] = split(x_v[...])
        c_x.wait_recv()
        x_h[TOK:, :], x_l[TOK:, :] = split(xs_v[...])

    def split_w_in(n):
        l_wi[n].wait()
        wi_h[n], wi_l[n] = split(wi_v[n])

    QR = ROWS // 2

    def y_copy(t, m):
        return remote(ysend.at[t, m], yrecv.at[t, m], yss.at[t, m], yrs.at[t, m], y_next if m % 2 == 0 else y_prev)

    def y_block(t, n):
        rows = pl.ds(t * ROWS, ROWS)
        return dot3((hid_h[rows, :], hid_l[rows, :]), (wi_h[n], wi_l[n]), NT)

    def y_send(t, m, value):
        ysend[t, m] = value
        y_copy(t, m).start()

    def y_first(t):
        v = y_block(t, 0)
        y_send(t, 1, v[:QR])
        y_send(t, 0, v[QR:])

    def y_second(t):
        v = y_block(t, 1)
        y_send(t, 2, v[:QR])
        ysend[t, 4] = v[QR:]
        v = y_block(t, 2)
        y_send(t, 3, v[QR:])
        ysend[t, 5] = v[:QR]

    def y_third(t):
        for m in (4, 5):
            y_copy(t, m - 4).wait_recv()
            ysend[t, m] = ysend[t, m] + yrecv[t, m - 4]
            y_copy(t, m).start()

    def y_own(t):
        yown[t] = y_block(t, 3)

    def v_copy(t):
        return remote(hsnd.at[t], hrcv.at[t], vss.at[t], vrs.at[t], partner)

    def y_final(t):
        for h, ms in ((0, (2, 5)), (1, (3, 4))):
            for m in ms:
                y_copy(t, m).wait_recv()
            rows = pl.ds(h * QR, QR)
            total = yown[t, rows] + yrecv[t, ms[0]] + yrecv[t, ms[1]]
            low, high = total[:, :BLK], total[:, BLK:]
            hsnd[t, rows] = jnp.where(zh == 0, high, low)
            gi_v[pl.ds(t * ROWS + h * QR, QR), :] = jnp.where(zh == 0, low, high)
        v_copy(t).start()

    def v_final(t):
        v_copy(t).wait_recv()
        rows = pl.ds(t * ROWS, ROWS)
        gi_v[rows, :] = gi_v[rows, :] + hrcv[t]

    l_g.wait()
    g_h[:TOK, :], g_l[:TOK, :] = split(g_v[...])
    partial(0)
    z_step(0)
    partial(1)
    z_step_own = z_step
    gelu(0)
    for h in range(2):
        c_g[h].wait_recv()
        half = pl.ds(h * HALF, HALF)
        g_h[TOK:, half], g_l[TOK:, half] = split(gs_v[h])
    x_first(0)
    z_step(1)
    partial(2)
    z_step(2)
    partial(3)
    gelu(1)
    gelu(2)
    x_second(0)
    z_step(3)
    x_third_local(0)
    z_step(4)
    gelu(3)
    z_step(5)
    x_third(0)
    z_step(6)
    x_own(0)
    z_step(7)
    split_w_in(0)
    z_step(8)
    split_w_in(1)
    z_step(9)
    split_w_in(2)
    z_step(10)
    split_w_in(3)
    z_step(11)
    split_inputs()
    z_step(12)
    y_first(0)
    z_step(13)
    y_second(0)
    z_step(14)
    hidden_sibling(0)
    x_first(1)
    y_third(0)
    z_step(15)
    x_final(0)
    z_step(16)
    y_own(0)
    z_step(17)
    z_step(18)
    hidden_sibling(1)
    hidden_sibling(2)
    x_second(1)
    z_step(19)
    z_step(20)
    y_first(1)
    y_second(1)
    x_third_local(1)
    x_third(1)
    y_third(1)
    y_final(0)
    hidden_sibling(3)
    x_own(1)
    y_own(1)
    v_final(0)
    y_final(1)
    x_final(1)
    v_final(1)
    out = pltpu.make_async_copy(gi_v, gi_out, osem.at[2])
    out.start()

    n = len(CHUNKS)
    for i in range(n):
        @pl.when((gx == 1) | (gx == 2) | ((gx == 0) & (i >= n - FLIGHT)))
        def _():
            right(i).wait_send()

        @pl.when((gx == 1) | (gx == 2) | ((gx == 3) & (i >= n - FLIGHT)))
        def _():
            left(i).wait_send()

    for copy in (*c_p, *c_g, c_x, *c_h):
        copy.wait_send()
    for m in range(6):
        for g in range(2):
            x_copy(g, m).wait_send()
        for t in range(PARTS):
            y_copy(t, m).wait_send()
    for t in range(PARTS):
        v_copy(t).wait_send()
    pltpu.make_async_copy(gwo_v, gwo_out, osem.at[0]).wait()
    pltpu.make_async_copy(gwi_v, gwi_out, osem.at[1]).wait()
    out.wait()


def per_device(inputs, pre_act, w_in, w_out, grad_out):
    v = pltpu.VMEM
    dma = pltpu.SemaphoreType.DMA
    scratch = [
        v((TOK, WID), F32), v((2, TOK, HALF), F32), v((2 * TOK, WID), BF16), v((2 * TOK, WID), BF16),
        v((8, BLK, WID), F32), v((WID, WID), BF16), v((WID, WID), BF16),
        v((4, TOK, WID), F32), v((4, TOK, WID), BF16), v((4, TOK, WID), BF16),
        v((TOK, WID), F32), v((TOK, WID), F32), v((2 * TOK, WID), BF16), v((2 * TOK, WID), BF16),
        v((8, TOK, BLK), F32), v((4, TOK, BLK), F32), v((8, TOK, BLK), F32),
        v((4, BLK, 2 * TOK), BF16), v((4, BLK, 2 * TOK), BF16), v((4, BLK, 2 * TOK), BF16), v((4, BLK, 2 * TOK), BF16),
        *[v((8, TOK, BLK), F32)] * 5,
        v((TOK, WID), BF16), v((TOK, WID), BF16), v((4, TOK, BLK), F32), v((4, TOK, BLK), F32),
        v((2, 6, BLK, HALF), F32), v((2, 6, BLK, HALF), F32), v((2, 2, BLK, HALF), F32),
        v((PARTS, 6, ROWS // 2, 2 * BLK), F32), v((PARTS, 6, ROWS // 2, 2 * BLK), F32), v((PARTS, ROWS, 2 * BLK), F32),
        v((PARTS, ROWS, BLK), F32), v((PARTS, ROWS, BLK), F32),
        v((TOK, BLK), F32), v((WID, BLK), F32), v((BLK, WID), F32),
        dma((22,)), dma((3,)), dma((11,)), dma((11,)), dma((2, len(CHUNKS))), dma((2, len(CHUNKS))),
        dma((2, 6)), dma((2, 6)), dma((PARTS, 6)), dma((PARTS, 6)), dma((PARTS,)), dma((PARTS,)),
    ]
    return pl.pallas_call(
        kernel,
        out_shape=(
            jax.ShapeDtypeStruct((TOK, BLK), F32),
            jax.ShapeDtypeStruct((WID, BLK), F32),
            jax.ShapeDtypeStruct((BLK, WID), F32),
        ),
        in_specs=[pl.BlockSpec(memory_space=pl.ANY)] * 5,
        out_specs=[pl.BlockSpec(memory_space=pl.ANY)] * 3,
        scratch_shapes=scratch,
        compiler_params=pltpu.CompilerParams(collective_id=0, has_side_effects=True, vmem_limit_bytes=60 << 20),
        cost_estimate=pl.CostEstimate(flops=6_442_450_944, bytes_accessed=13 << 20, transcendentals=1 << 19),
        name="mlp_backward",
    )(inputs, pre_act, w_in, w_out, grad_out)


def solution(mesh):
    in_specs = (P("gz", "gx"), P("gz", "gy"), P("gx", "gy"), P("gy", "gx"), P("gz", "gx"))
    out_specs = (P("gz", ("gx", "gy")), P("gx", ("gy", "gz")), P(("gy", "gz"), "gx"))
    return jax.shard_map(
        per_device, mesh=mesh, in_specs=in_specs, out_specs=out_specs, check_vma=False
    )
```

```python
import functools

import jax
import jax.numpy as jnp
from jax import lax
from jax.experimental import pallas as pl
from jax.experimental.pallas import tpu as pltpu
from jax.sharding import PartitionSpec as P

MESH = pl.DeviceIdType.MESH
F32 = jnp.float32
BF16 = jnp.bfloat16
sqrt_two_pi = 0.7978845608028654
cubic_coef = 0.044715

TOK = 256
WID = 1024
BLK = 128
HALF = 512
PARTS = 2
ROWS = TOK // PARTS
SUB = 64
CHUNKS = [(k, e, r) for t in range(PARTS) for k in range(4) for e in range(2) for r in range(t * ROWS, (t + 1) * ROWS, SUB)]
LAG = 5
AHEAD = 4
FLIGHT = 6

NN = (((1,), (0,)), ((), ()))
NT = (((1,), (1,)), ((), ()))


def split(value):
    high = value.astype(BF16)
    return high, (value - high.astype(F32)).astype(BF16)


def dot3(left, right, dims):
    (lh, ll), (rh, rl) = left, right
    d = lambda a, b: lax.dot_general(a, b, dims, preferred_element_type=F32)
    return d(lh, rh) + (d(lh, rl) + d(ll, rh))


def tangent_of(v):
    return jnp.tanh(sqrt_two_pi * (v + cubic_coef * v * v * v))


def gelu_value(v, t):
    return 0.5 * v * (1.0 + t)


def gelu_slope(v, t):
    return 0.5 * (1.0 + t) + 0.5 * v * (1.0 - t * t) * sqrt_two_pi * (1.0 + 3.0 * cubic_coef * v * v)


def kernel(
    x_in, p_in, wi_in, wo_in, g_in, gi_v, gwi_v, gwo_v,
    g_v, gs_v, g_h, g_l, wo_v, wo_h, wo_l, wi_v, wi_h, wi_l, x_v, xs_v, x_h, x_l,
    p_v, ps_v, der_v, a_h, a_l, h_h, h_l, own_z, rp, rs, sp, ss, hid_h, hid_l, hsend, hs_v,
    xsend, xrecv, xown, ysend, yrecv, yown, hsnd, hrcv,
    lsem, csend, crecv, zsend, zrecv, xss, xrs, yss, yrs, vss, vrs,
):
    gx, gy, gz = lax.axis_index("gx"), lax.axis_index("gy"), lax.axis_index("gz")
    y, zh, x, c = gy // 2, gy % 2, gz // 2, gz % 2
    xp, xm, xo = (x + 1) % 4, (x + 3) % 4, (x + 2) % 4
    yp, ym, yo = (y + 1) % 4, (y + 3) % 4, (y + 2) % 4
    owners = (xo, xp, xm, x)
    yowners = (yo, yp, ym, y)
    sibling = (gx, gy, x * 2 + 1 - c)
    x_next, x_prev = (gx, gy, xp * 2 + c), (gx, gy, xm * 2 + c)
    y_next, y_prev = (gx, yp * 2 + zh, gz), (gx, ym * 2 + zh, gz)
    partner = (gx, y * 2 + 1 - zh, gz)
    zr, zl = (gx + 1) % 4, (gx + 3) % 4
    z_next = (zr, y * 2 + jnp.where(gx == 3, 1 - zh, zh), gz)
    z_prev = (zl, y * 2 + jnp.where(gx == 0, 1 - zh, zh), gz)

    def block(k, e):
        return 2 * owners[k] + (c if e else 1 - c)

    def cols(k, e):
        return pl.ds(pl.multiple_of(block(k, e) * BLK, BLK), BLK)

    def load(src, dst, n):
        return pltpu.make_async_copy(src, dst, lsem.at[n])

    l_g = load(g_in, g_v, 0)
    l_wo = [[load(wo_in.at[cols(k, e), :], wo_v.at[2 * k + e], 1 + 2 * k + e) for e in range(2)] for k in range(4)]
    l_p = [[load(p_in.at[:, cols(k, e)], p_v.at[2 * k + e], 9 + 2 * k + e) for e in range(2)] for k in range(4)]
    l_x = load(x_in, x_v, 17)
    l_wi = [
        load(wi_in.at[pl.ds(pl.multiple_of(yowners[n] * TOK, TOK), TOK), :], wi_v.at[n], 18 + n) for n in range(4)
    ]
    l_g.start()
    for k in range(4):
        for e in range(2):
            l_wo[k][e].start()
        if k == 0:
            for j in range(4):
                for e in range(2):
                    l_p[j][e].start()
    l_x.start()
    for n in range(4):
        l_wi[n].start()

    barrier = pltpu.get_barrier_semaphore()
    for who in (sibling, x_next, x_prev, y_next, y_prev, z_next, z_prev, partner):
        pl.semaphore_signal(barrier, inc=1, device_id=who, device_id_type=MESH)
    pl.semaphore_wait(barrier, 8)

    def remote(src, dst, s_sem, r_sem, who):
        return pltpu.make_async_remote_copy(
            src_ref=src, dst_ref=dst, send_sem=s_sem, recv_sem=r_sem, device_id=who, device_id_type=MESH
        )

    c_p = [remote(p_in.at[:, cols(k, 0)], ps_v.at[k], csend.at[k], crecv.at[k], sibling) for k in range(4)]
    c_g = [
        remote(g_in.at[:, pl.ds(h * HALF, HALF)], gs_v.at[h], csend.at[4 + h], crecv.at[4 + h], sibling)
        for h in range(2)
    ]
    c_x = remote(x_in, xs_v, csend.at[6], crecv.at[6], sibling)
    c_h = [remote(hsend.at[k], hs_v.at[k], csend.at[7 + k], crecv.at[7 + k], sibling) for k in range(4)]
    c_p[0].start()
    c_g[0].start()
    c_g[1].start()
    for k in range(1, 4):
        c_p[k].start()
    c_x.start()

    @pl.when(gx == 0)
    def _():
        rp[...] = jnp.zeros_like(rp)

    @pl.when(gx == 3)
    def _():
        rs[...] = jnp.zeros_like(rs)

    def where(i):
        k, e, r = CHUNKS[i]
        return (2 * k + e, pl.ds(r, SUB))

    def z_copy(src, dst, way, i):
        b, rows = where(i)
        return remote(
            src.at[b, rows], dst.at[b, rows], zsend.at[way, i], zrecv.at[way, i], z_next if way == 0 else z_prev
        )

    def right(i, src=None):
        return z_copy(sp if src is None else src, rp, 0, i)

    def left(i, src=None):
        return z_copy(ss if src is None else src, rs, 1, i)

    def z_own(i):
        @pl.when(gx == 0)
        def _():
            if i >= FLIGHT:
                right(i - FLIGHT).wait_send()
            right(i, own_z).start()

        @pl.when(gx == 3)
        def _():
            if i >= FLIGHT:
                left(i - FLIGHT).wait_send()
            left(i, own_z).start()

    def forward_right(i):
        b, rows = where(i)
        right(i).wait_recv()
        sp[b, rows] = own_z[b, rows] + rp[b, rows]
        right(i).start()

    def forward_left(i):
        b, rows = where(i)
        left(i).wait_recv()
        ss[b, rows] = own_z[b, rows] + rs[b, rows]
        left(i).start()

    def z_near(i):
        pl.when(gx == 1)(lambda: forward_right(i))
        pl.when(gx == 2)(lambda: forward_left(i))

    def z_far(i):
        pl.when(gx == 1)(lambda: forward_left(i))
        pl.when(gx == 2)(lambda: forward_right(i))

    def z_final(i):
        k, e, r = CHUNKS[i]
        b, rows = where(i)

        @pl.when(gx == 0)
        def _():
            left(i).wait_recv()

        @pl.when(gx == 3)
        def _():
            right(i).wait_recv()

        hidden = (own_z[b, rows] + rp[b, rows] + rs[b, rows]) * der_v[b, rows]
        high, low = split(hidden)
        hid_h[rows, cols(k, e)] = high
        hid_l[rows, cols(k, e)] = low
        if e == 0:
            hsend[k, rows] = hidden
            if r + SUB == TOK:
                c_h[k].start()
        else:
            high, low = split(hidden.T)
            h_h[k, :, rows] = high
            h_l[k, :, rows] = low

    n_chunks = len(CHUNKS)

    def z_group(j):
        for i in (2 * j, 2 * j + 1):
            if AHEAD <= i + AHEAD < n_chunks:
                z_own(i + AHEAD)
            if i < n_chunks:
                z_near(i)
            if 0 <= i - LAG < n_chunks:
                z_far(i - LAG)
            if 0 <= i - 2 * LAG < n_chunks:
                z_final(i - 2 * LAG)

    def partial(k):
        for e in range(2):
            l_wo[k][e].wait()
            b = 2 * k + e
            wo_h[pl.ds(b * BLK, BLK), :], wo_l[pl.ds(b * BLK, BLK), :] = split(wo_v[b])
        rows = pl.ds(2 * k * BLK, 2 * BLK)
        value = dot3((g_h[:TOK, :], g_l[:TOK, :]), (wo_h[rows, :], wo_l[rows, :]), NT)
        own_z[2 * k] = value[:, :BLK]
        own_z[2 * k + 1] = value[:, BLK:]

    def gelu(k):
        for e in range(2):
            l_p[k][e].wait()
            v = p_v[2 * k + e]
            t = tangent_of(v)
            der_v[2 * k + e] = gelu_slope(v, t)
            if e == 1:
                a_h[k, :, :TOK], a_l[k, :, :TOK] = split(gelu_value(v, t).T)
        c_p[k].wait_recv()
        v = ps_v[k]
        a_h[k, :, TOK:], a_l[k, :, TOK:] = split(gelu_value(v, tangent_of(v)).T)

    def x_copy(g, m):
        return remote(xsend.at[g, m], xrecv.at[g, m], xss.at[g, m], xrs.at[g, m], x_next if m % 2 == 0 else x_prev)

    def weight(g, k, h):
        th, tl, vh, vl = (a_h, a_l, g_h, g_l) if g == 0 else (h_h, h_l, x_h, x_l)
        half = pl.ds(h * HALF, HALF)
        return dot3((th[k], tl[k]), (vh[:, half], vl[:, half]), NN)

    def x_send(g, m, k, h):
        xsend[g, m] = weight(g, k, h)
        x_copy(g, m).start()

    def x_first(g):
        x_send(g, 1, 0, 0)
        x_send(g, 0, 0, 1)

    def x_second(g):
        x_send(g, 2, 1, 0)
        x_send(g, 3, 2, 1)

    def x_third_local(g):
        xsend[g, 4] = weight(g, 1, 1)
        xsend[g, 5] = weight(g, 2, 0)

    def x_third(g):
        for m in (4, 5):
            x_copy(g, m - 4).wait_recv()
            xsend[g, m] = xsend[g, m] + xrecv[g, m - 4]
            x_copy(g, m).start()

    def x_own(g):
        xown[g, 0] = weight(g, 3, 0)
        xown[g, 1] = weight(g, 3, 1)

    def x_final(g):
        for h, ms in ((0, (2, 5)), (1, (3, 4))):
            for m in ms:
                x_copy(g, m).wait_recv()
            total = xown[g, h] + xrecv[g, ms[0]] + xrecv[g, ms[1]]
            half = pl.ds(h * HALF, HALF)
            if g == 0:
                gwo_v[:, half] = total
            else:
                gwi_v[half, :] = total.T

    def hidden_sibling(k):
        c_h[k].wait_recv()
        h_h[k, :, TOK:], h_l[k, :, TOK:] = split(hs_v[k].T)

    def split_inputs():
        l_x.wait()
        x_h[:TOK, :], x_l[:TOK, :] = split(x_v[...])
        c_x.wait_recv()
        x_h[TOK:, :], x_l[TOK:, :] = split(xs_v[...])

    def split_w_in(n):
        l_wi[n].wait()
        wi_h[n], wi_l[n] = split(wi_v[n])

    QR = ROWS // 2

    def y_copy(t, m):
        return remote(ysend.at[t, m], yrecv.at[t, m], yss.at[t, m], yrs.at[t, m], y_next if m % 2 == 0 else y_prev)

    def y_block(t, n):
        rows = pl.ds(t * ROWS, ROWS)
        return dot3((hid_h[rows, :], hid_l[rows, :]), (wi_h[n], wi_l[n]), NT)

    def y_send(t, m, value):
        ysend[t, m] = value
        y_copy(t, m).start()

    def y_first(t):
        v = y_block(t, 0)
        y_send(t, 1, v[:QR])
        y_send(t, 0, v[QR:])

    def y_second(t):
        v = y_block(t, 1)
        y_send(t, 2, v[:QR])
        ysend[t, 4] = v[QR:]
        v = y_block(t, 2)
        y_send(t, 3, v[QR:])
        ysend[t, 5] = v[:QR]

    def y_third(t):
        for m in (4, 5):
            y_copy(t, m - 4).wait_recv()
            ysend[t, m] = ysend[t, m] + yrecv[t, m - 4]
            y_copy(t, m).start()

    def y_own(t):
        yown[t] = y_block(t, 3)

    def v_copy(t):
        return remote(hsnd.at[t], hrcv.at[t], vss.at[t], vrs.at[t], partner)

    def y_final(t):
        for h, ms in ((0, (2, 5)), (1, (3, 4))):
            for m in ms:
                y_copy(t, m).wait_recv()
            rows = pl.ds(h * QR, QR)
            total = yown[t, rows] + yrecv[t, ms[0]] + yrecv[t, ms[1]]
            low, high = total[:, :BLK], total[:, BLK:]
            hsnd[t, rows] = jnp.where(zh == 0, high, low)
            gi_v[pl.ds(t * ROWS + h * QR, QR), :] = jnp.where(zh == 0, low, high)
        v_copy(t).start()

    def v_final(t):
        v_copy(t).wait_recv()
        rows = pl.ds(t * ROWS, ROWS)
        gi_v[rows, :] = gi_v[rows, :] + hrcv[t]

    l_g.wait()
    g_h[:TOK, :], g_l[:TOK, :] = split(g_v[...])
    partial(0)
    for i in range(AHEAD):
        z_own(i)
    gelu(0)
    for h in range(2):
        c_g[h].wait_recv()
        half = pl.ds(h * HALF, HALF)
        g_h[TOK:, half], g_l[TOK:, half] = split(gs_v[h])
    x_first(0)
    partial(1)
    z_group(0)
    partial(2)
    z_group(1)
    partial(3)
    z_group(2)
    gelu(1)
    z_group(3)
    gelu(2)
    z_group(4)
    x_second(0)
    z_group(5)
    x_third_local(0)
    z_group(6)
    gelu(3)
    z_group(7)
    x_third(0)
    z_group(8)
    x_own(0)
    z_group(9)
    split_w_in(0)
    z_group(10)
    split_w_in(1)
    z_group(11)
    split_w_in(2)
    z_group(12)
    y_first(0)
    z_group(13)
    split_w_in(3)
    z_group(14)
    y_second(0)
    z_group(15)
    split_inputs()
    z_group(16)
    y_third(0)
    hidden_sibling(0)
    x_first(1)
    z_group(17)
    y_own(0)
    z_group(18)
    z_group(19)
    hidden_sibling(1)
    hidden_sibling(2)
    x_second(1)
    x_third_local(1)
    z_group(20)
    y_first(1)
    y_second(1)
    x_third(1)
    y_third(1)
    y_final(0)
    y_own(1)
    x_final(0)
    hidden_sibling(3)
    x_own(1)
    v_final(0)
    y_final(1)
    x_final(1)
    v_final(1)

    n = n_chunks
    for i in range(n):
        @pl.when((gx == 1) | (gx == 2) | ((gx == 0) & (i >= n - FLIGHT)))
        def _():
            right(i).wait_send()

        @pl.when((gx == 1) | (gx == 2) | ((gx == 3) & (i >= n - FLIGHT)))
        def _():
            left(i).wait_send()

    for copy in (*c_p, *c_g, c_x, *c_h):
        copy.wait_send()
    for m in range(6):
        for g in range(2):
            x_copy(g, m).wait_send()
        for t in range(PARTS):
            y_copy(t, m).wait_send()
    for t in range(PARTS):
        v_copy(t).wait_send()


def write_out(*refs):
    copies = [pltpu.make_async_copy(refs[n], refs[3 + n], refs[6].at[n]) for n in range(3)]
    for copy in copies:
        copy.start()
    for copy in copies:
        copy.wait()


def per_device(inputs, pre_act, w_in, w_out, grad_out):
    v = pltpu.VMEM
    dma = pltpu.SemaphoreType.DMA
    scratch = [
        v((TOK, WID), F32), v((2, TOK, HALF), F32), v((2 * TOK, WID), BF16), v((2 * TOK, WID), BF16),
        v((8, BLK, WID), F32), v((WID, WID), BF16), v((WID, WID), BF16),
        v((4, TOK, WID), F32), v((4, TOK, WID), BF16), v((4, TOK, WID), BF16),
        v((TOK, WID), F32), v((TOK, WID), F32), v((2 * TOK, WID), BF16), v((2 * TOK, WID), BF16),
        v((8, TOK, BLK), F32), v((4, TOK, BLK), F32), v((8, TOK, BLK), F32),
        v((4, BLK, 2 * TOK), BF16), v((4, BLK, 2 * TOK), BF16), v((4, BLK, 2 * TOK), BF16), v((4, BLK, 2 * TOK), BF16),
        *[v((8, TOK, BLK), F32)] * 5,
        v((TOK, WID), BF16), v((TOK, WID), BF16), v((4, TOK, BLK), F32), v((4, TOK, BLK), F32),
        v((2, 6, BLK, HALF), F32), v((2, 6, BLK, HALF), F32), v((2, 2, BLK, HALF), F32),
        v((PARTS, 6, ROWS // 2, 2 * BLK), F32), v((PARTS, 6, ROWS // 2, 2 * BLK), F32), v((PARTS, ROWS, 2 * BLK), F32),
        v((PARTS, ROWS, BLK), F32), v((PARTS, ROWS, BLK), F32),
        dma((22,)), dma((11,)), dma((11,)), dma((2, len(CHUNKS))), dma((2, len(CHUNKS))),
        dma((2, 6)), dma((2, 6)), dma((PARTS, 6)), dma((PARTS, 6)), dma((PARTS,)), dma((PARTS,)),
    ]
    results = pl.pallas_call(
        kernel,
        out_shape=(v((TOK, BLK), F32), v((WID, BLK), F32), v((BLK, WID), F32)),
        in_specs=[pl.BlockSpec(memory_space=pl.ANY)] * 5,
        out_specs=[pl.BlockSpec(memory_space=pltpu.VMEM)] * 3,
        scratch_shapes=scratch,
        compiler_params=pltpu.CompilerParams(collective_id=0, has_side_effects=True, vmem_limit_bytes=60 << 20),
        cost_estimate=pl.CostEstimate(flops=6_442_450_944, bytes_accessed=13 << 20, transcendentals=1 << 19),
        name="mlp_backward",
    )(inputs, pre_act, w_in, w_out, grad_out)
    return pl.pallas_call(
        write_out,
        out_shape=[jax.ShapeDtypeStruct(r.shape, F32) for r in results],
        in_specs=[pl.BlockSpec(memory_space=pl.ANY)] * 3,
        out_specs=[pl.BlockSpec(memory_space=pl.ANY)] * 3,
        scratch_shapes=[dma((3,))],
        compiler_params=pltpu.CompilerParams(vmem_limit_bytes=2 << 20),
        name="write_out",
    )(*results)


def solution(mesh):
    in_specs = (P("gz", "gx"), P("gz", "gy"), P("gx", "gy"), P("gy", "gx"), P("gz", "gx"))
    out_specs = (P("gz", ("gx", "gy")), P("gx", ("gy", "gz")), P(("gy", "gz"), "gx"))
    return jax.shard_map(
        per_device, mesh=mesh, in_specs=in_specs, out_specs=out_specs, check_vma=False
    )
```

```python
import functools

import jax
import jax.numpy as jnp
from jax import lax
from jax.experimental import pallas as pl
from jax.experimental.pallas import tpu as pltpu
from jax.sharding import PartitionSpec as P

MESH = pl.DeviceIdType.MESH
F32 = jnp.float32
BF16 = jnp.bfloat16
sqrt_two_pi = 0.7978845608028654
cubic_coef = 0.044715

TOK = 256
WID = 1024
BLK = 128
HALF = 512
PARTS = 2
ROWS = TOK // PARTS
SUB = 64
CHUNKS = [(k, e, r) for t in range(PARTS) for k in range(4) for e in range(2) for r in range(t * ROWS, (t + 1) * ROWS, SUB)]
LAG = 5
AHEAD = 4
FLIGHT = 6

NN = (((1,), (0,)), ((), ()))
NT = (((1,), (1,)), ((), ()))


def split(value):
    high = value.astype(BF16)
    return high, (value - high.astype(F32)).astype(BF16)


def dot3(left, right, dims):
    (lh, ll), (rh, rl) = left, right
    d = lambda a, b: lax.dot_general(a, b, dims, preferred_element_type=F32)
    return d(lh, rh) + (d(lh, rl) + d(ll, rh))


def tangent_of(v):
    return jnp.tanh(sqrt_two_pi * (v + cubic_coef * v * v * v))


def gelu_value(v, t):
    return 0.5 * v * (1.0 + t)


def gelu_slope(v, t):
    return 0.5 * (1.0 + t) + 0.5 * v * (1.0 - t * t) * sqrt_two_pi * (1.0 + 3.0 * cubic_coef * v * v)


def kernel(
    x_in, p_in, wi_in, wo_in, g_in, gi_v, gwi_v, gwo_v,
    g_v, gs_v, g_h, g_l, wo_v, wo_h, wo_l, wi_v, wi_h, wi_l, x_v, xs_v, x_h, x_l,
    p_v, ps_v, der_v, a_h, a_l, h_h, h_l, own_z, rp, rs, sp, ss, hid_h, hid_l, hsend, hs_v,
    xsend, xrecv, xown, ysend, yrecv, yown, hsnd, hrcv,
    lsem, csend, crecv, zsend, zrecv, xss, xrs, yss, yrs, vss, vrs, core_in, z_in, v_in,
):
    gx, gy, gz = lax.axis_index("gx"), lax.axis_index("gy"), lax.axis_index("gz")
    y, zh, x, c = gy // 2, gy % 2, gz // 2, gz % 2
    xp, xm, xo = (x + 1) % 4, (x + 3) % 4, (x + 2) % 4
    yp, ym, yo = (y + 1) % 4, (y + 3) % 4, (y + 2) % 4
    owners = (xo, xp, xm, x)
    yowners = (yo, yp, ym, y)
    sibling = (gx, gy, x * 2 + 1 - c)
    x_next, x_prev = (gx, gy, xp * 2 + c), (gx, gy, xm * 2 + c)
    y_next, y_prev = (gx, yp * 2 + zh, gz), (gx, ym * 2 + zh, gz)
    partner = (gx, y * 2 + 1 - zh, gz)
    z_next, z_prev = ((gx + 1) % 4, gy, gz), ((gx + 3) % 4, gy, gz)

    def block(k, e):
        return 2 * owners[k] + (c if e else 1 - c)

    def cols(k, e):
        return pl.ds(pl.multiple_of(block(k, e) * BLK, BLK), BLK)

    def load(src, dst, n):
        return pltpu.make_async_copy(src, dst, lsem.at[n])

    l_g = load(g_in, g_v, 0)
    l_wo = [[load(wo_in.at[cols(k, e), :], wo_v.at[2 * k + e], 1 + 2 * k + e) for e in range(2)] for k in range(4)]
    l_p = [[load(p_in.at[:, cols(k, e)], p_v.at[2 * k + e], 9 + 2 * k + e) for e in range(2)] for k in range(4)]
    l_x = load(x_in, x_v, 17)
    l_wi = [
        load(wi_in.at[pl.ds(pl.multiple_of(yowners[n] * TOK, TOK), TOK), :], wi_v.at[n], 18 + n) for n in range(4)
    ]
    l_g.start()
    for k in range(4):
        for e in range(2):
            l_wo[k][e].start()
        if k == 0:
            for j in range(4):
                for e in range(2):
                    l_p[j][e].start()
    l_x.start()
    for n in range(4):
        l_wi[n].start()

    barrier = pltpu.get_barrier_semaphore()
    def tell(sem, who):
        pl.semaphore_signal(sem, inc=1, device_id=who, device_id_type=MESH)

    for who in (x_next, x_prev, y_next, y_prev):
        tell(barrier, who)
    pl.when(c == 0)(lambda: tell(barrier, sibling))
    pl.when(gx < 3)(lambda: tell(barrier, z_next))
    pl.when(zh == 0)(lambda: tell(barrier, partner))
    pl.semaphore_wait(barrier, 4 + c + jnp.where(gx > 0, 1, 0) + zh)
    pl.when(c == 1)(lambda: tell(core_in, sibling))
    pl.when(gx > 0)(lambda: tell(z_in, z_prev))
    pl.when(zh == 1)(lambda: tell(v_in, partner))

    def remote(src, dst, s_sem, r_sem, who):
        return pltpu.make_async_remote_copy(
            src_ref=src, dst_ref=dst, send_sem=s_sem, recv_sem=r_sem, device_id=who, device_id_type=MESH
        )

    c_p = [remote(p_in.at[:, cols(k, 0)], ps_v.at[k], csend.at[k], crecv.at[k], sibling) for k in range(4)]
    c_g = [
        remote(g_in.at[:, pl.ds(h * HALF, HALF)], gs_v.at[h], csend.at[4 + h], crecv.at[4 + h], sibling)
        for h in range(2)
    ]
    c_x = remote(x_in, xs_v, csend.at[6], crecv.at[6], sibling)
    c_h = [remote(hsend.at[k], hs_v.at[k], csend.at[7 + k], crecv.at[7 + k], sibling) for k in range(4)]
    def greet_sibling():
        pl.when(c == 0)(lambda: pl.semaphore_wait(core_in, 1))
        c_p[0].start()
        c_g[0].start()
        c_g[1].start()
        for k in range(1, 4):
            c_p[k].start()
        c_x.start()

    @pl.when(gx == 0)
    def _():
        rp[...] = jnp.zeros_like(rp)

    @pl.when(gx == 3)
    def _():
        rs[...] = jnp.zeros_like(rs)

    def where(i):
        k, e, r = CHUNKS[i]
        return (2 * k + e, pl.ds(r, SUB))

    def z_copy(src, dst, way, i):
        b, rows = where(i)
        return remote(
            src.at[b, rows], dst.at[b, rows], zsend.at[way, i], zrecv.at[way, i], z_next if way == 0 else z_prev
        )

    def right(i, src=None):
        return z_copy(sp if src is None else src, rp, 0, i)

    def left(i, src=None):
        return z_copy(ss if src is None else src, rs, 1, i)

    def z_own(send, i):
        if i < n_chunks:
            if i >= FLIGHT:
                send(i - FLIGHT).wait_send()
            send(i, own_z).start()

    def forward(send, total, came, i):
        if 0 <= i < n_chunks:
            b, rows = where(i)
            send(i).wait_recv()
            total[b, rows] = own_z[b, rows] + came[b, rows]
            send(i).start()

    def z_begin():
        @pl.when(gx == 0)
        def _():
            pl.semaphore_wait(z_in, 1)
            for i in range(AHEAD):
                z_own(right, i)

        @pl.when(gx == 3)
        def _():
            for i in range(AHEAD):
                z_own(left, i)

        @pl.when((gx == 1) | (gx == 2))
        def _():
            pl.semaphore_wait(z_in, 1)

    n_chunks = len(CHUNKS)

    def z_group(j):
        pair = (2 * j, 2 * j + 1)
        last = [i - 2 * LAG for i in pair if 0 <= i - 2 * LAG < n_chunks]

        @pl.when(gx == 0)
        def _():
            for i in pair:
                z_own(right, i + AHEAD)
            for i in last:
                left(i).wait_recv()

        @pl.when(gx == 1)
        def _():
            for i in pair:
                forward(right, sp, rp, i)
                forward(left, ss, rs, i - LAG)

        @pl.when(gx == 2)
        def _():
            for i in pair:
                forward(left, ss, rs, i)
                forward(right, sp, rp, i - LAG)

        @pl.when(gx == 3)
        def _():
            for i in pair:
                z_own(left, i + AHEAD)
            for i in last:
                right(i).wait_recv()

        if last:
            k, e, r = CHUNKS[last[0]]
            b, rows = 2 * k + e, pl.ds(r, 2 * SUB)
            hidden = (own_z[b, rows] + rp[b, rows] + rs[b, rows]) * der_v[b, rows]
            high, low = split(hidden)
            hid_h[rows, cols(k, e)] = high
            hid_l[rows, cols(k, e)] = low
            if e == 0:
                hsend[k, rows] = hidden
                if r + 2 * SUB == TOK:
                    c_h[k].start()
            else:
                high, low = split(hidden.T)
                h_h[k, :, rows] = high
                h_l[k, :, rows] = low

    def partial(k):
        for e in range(2):
            l_wo[k][e].wait()
            b = 2 * k + e
            wo_h[pl.ds(b * BLK, BLK), :], wo_l[pl.ds(b * BLK, BLK), :] = split(wo_v[b])
        rows = pl.ds(2 * k * BLK, 2 * BLK)
        value = dot3((g_h[:TOK, :], g_l[:TOK, :]), (wo_h[rows, :], wo_l[rows, :]), NT)
        own_z[2 * k] = value[:, :BLK]
        own_z[2 * k + 1] = value[:, BLK:]

    def gelu(k):
        for e in range(2):
            l_p[k][e].wait()
            v = p_v[2 * k + e]
            t = tangent_of(v)
            der_v[2 * k + e] = gelu_slope(v, t)
            if e == 1:
                a_h[k, :, :TOK], a_l[k, :, :TOK] = split(gelu_value(v, t).T)
        if k > 0:
            gelu_sibling(k)

    def gelu_sibling(k):
        c_p[k].wait_recv()
        v = ps_v[k]
        a_h[k, :, TOK:], a_l[k, :, TOK:] = split(gelu_value(v, tangent_of(v)).T)

    def x_copy(g, m):
        return remote(xsend.at[g, m], xrecv.at[g, m], xss.at[g, m], xrs.at[g, m], x_next if m % 2 == 0 else x_prev)

    def weight(g, k, h):
        th, tl, vh, vl = (a_h, a_l, g_h, g_l) if g == 0 else (h_h, h_l, x_h, x_l)
        half = pl.ds(h * HALF, HALF)
        return dot3((th[k], tl[k]), (vh[:, half], vl[:, half]), NN)

    def x_send(g, m, k, h):
        xsend[g, m] = weight(g, k, h)
        x_copy(g, m).start()

    def x_first(g):
        x_send(g, 1, 0, 0)
        x_send(g, 0, 0, 1)

    def x_second(g):
        x_send(g, 2, 1, 0)
        x_send(g, 3, 2, 1)

    def x_third_local(g):
        xsend[g, 4] = weight(g, 1, 1)
        xsend[g, 5] = weight(g, 2, 0)

    def x_third(g):
        for m in (4, 5):
            x_copy(g, m - 4).wait_recv()
            xsend[g, m] = xsend[g, m] + xrecv[g, m - 4]
            x_copy(g, m).start()

    def x_own(g):
        xown[g, 0] = weight(g, 3, 0)
        xown[g, 1] = weight(g, 3, 1)

    def x_final(g):
        for h, ms in ((0, (2, 5)), (1, (3, 4))):
            for m in ms:
                x_copy(g, m).wait_recv()
            total = xown[g, h] + xrecv[g, ms[0]] + xrecv[g, ms[1]]
            half = pl.ds(h * HALF, HALF)
            if g == 0:
                gwo_v[:, half] = total
            else:
                gwi_v[half, :] = total.T

    def x_begin():
        gelu_sibling(0)
        for h in range(2):
            c_g[h].wait_recv()
            half = pl.ds(h * HALF, HALF)
            g_h[TOK:, half], g_l[TOK:, half] = split(gs_v[h])
        x_first(0)

    def hidden_sibling(k):
        c_h[k].wait_recv()
        h_h[k, :, TOK:], h_l[k, :, TOK:] = split(hs_v[k].T)

    def split_inputs():
        l_x.wait()
        x_h[:TOK, :], x_l[:TOK, :] = split(x_v[...])
        c_x.wait_recv()
        x_h[TOK:, :], x_l[TOK:, :] = split(xs_v[...])

    def split_w_in(n):
        l_wi[n].wait()
        wi_h[n], wi_l[n] = split(wi_v[n])

    QR = ROWS // 2

    def y_copy(t, m):
        return remote(ysend.at[t, m], yrecv.at[t, m], yss.at[t, m], yrs.at[t, m], y_next if m % 2 == 0 else y_prev)

    def y_block(t, n):
        rows = pl.ds(t * ROWS, ROWS)
        return dot3((hid_h[rows, :], hid_l[rows, :]), (wi_h[n], wi_l[n]), NT)

    def y_send(t, m, value):
        ysend[t, m] = value
        y_copy(t, m).start()

    def y_first(t):
        v = y_block(t, 0)
        y_send(t, 1, v[:QR])
        y_send(t, 0, v[QR:])

    def y_second(t):
        v = y_block(t, 1)
        y_send(t, 2, v[:QR])
        ysend[t, 4] = v[QR:]
        v = y_block(t, 2)
        y_send(t, 3, v[QR:])
        ysend[t, 5] = v[:QR]

    def y_third(t):
        for m in (4, 5):
            y_copy(t, m - 4).wait_recv()
            ysend[t, m] = ysend[t, m] + yrecv[t, m - 4]
            y_copy(t, m).start()

    def y_own(t):
        yown[t] = y_block(t, 3)

    def v_copy(t):
        return remote(hsnd.at[t], hrcv.at[t], vss.at[t], vrs.at[t], partner)

    def y_final(t):
        for h, ms in ((0, (2, 5)), (1, (3, 4))):
            for m in ms:
                y_copy(t, m).wait_recv()
            rows = pl.ds(h * QR, QR)
            total = yown[t, rows] + yrecv[t, ms[0]] + yrecv[t, ms[1]]
            low, high = total[:, :BLK], total[:, BLK:]
            hsnd[t, rows] = jnp.where(zh == 0, high, low)
            gi_v[pl.ds(t * ROWS + h * QR, QR), :] = jnp.where(zh == 0, low, high)
        if t == 0:
            pl.when(zh == 0)(lambda: pl.semaphore_wait(v_in, 1))
        v_copy(t).start()

    def v_final(t):
        v_copy(t).wait_recv()
        rows = pl.ds(t * ROWS, ROWS)
        gi_v[rows, :] = gi_v[rows, :] + hrcv[t]

    l_g.wait()
    g_h[:TOK, :], g_l[:TOK, :] = split(g_v[...])
    partial(0)
    z_begin()
    greet_sibling()
    gelu(0)
    pl.when(c == 1)(lambda: x_begin())
    partial(1)
    z_group(0)
    partial(2)
    pl.when(c == 0)(lambda: x_begin())
    z_group(1)
    partial(3)
    z_group(2)
    gelu(1)
    z_group(3)
    gelu(2)
    z_group(4)
    x_second(0)
    z_group(5)
    x_third_local(0)
    z_group(6)
    gelu(3)
    z_group(7)
    x_third(0)
    z_group(8)
    x_own(0)
    z_group(9)
    split_w_in(0)
    z_group(10)
    split_w_in(1)
    z_group(11)
    split_w_in(2)
    z_group(12)
    y_first(0)
    z_group(13)
    split_w_in(3)
    z_group(14)
    y_second(0)
    z_group(15)
    split_inputs()
    z_group(16)
    y_third(0)
    hidden_sibling(0)
    x_first(1)
    z_group(17)
    y_own(0)
    z_group(18)
    z_group(19)
    hidden_sibling(1)
    hidden_sibling(2)
    x_second(1)
    x_third_local(1)
    z_group(20)
    y_first(1)
    y_second(1)
    x_third(1)
    y_third(1)
    y_final(0)
    y_own(1)
    x_final(0)
    hidden_sibling(3)
    x_own(1)
    v_final(0)
    y_final(1)
    x_final(1)
    v_final(1)

    def all_left(sends, first=0):
        for i in range(first, n_chunks):
            for send in sends:
                send(i).wait_send()

    pl.when(gx == 0)(lambda: all_left((right,), n_chunks - FLIGHT))
    pl.when((gx == 1) | (gx == 2))(lambda: all_left((right, left)))
    pl.when(gx == 3)(lambda: all_left((left,), n_chunks - FLIGHT))
    for copy in (*c_p, *c_g, c_x, *c_h):
        copy.wait_send()
    for m in range(6):
        for g in range(2):
            x_copy(g, m).wait_send()
        for t in range(PARTS):
            y_copy(t, m).wait_send()
    for t in range(PARTS):
        v_copy(t).wait_send()


def write_out(*refs):
    copies = [pltpu.make_async_copy(refs[n], refs[3 + n], refs[6].at[n]) for n in range(3)]
    for copy in copies:
        copy.start()
    for copy in copies:
        copy.wait()


def per_device(inputs, pre_act, w_in, w_out, grad_out):
    v = pltpu.VMEM
    dma = pltpu.SemaphoreType.DMA
    scratch = [
        v((TOK, WID), F32), v((2, TOK, HALF), F32), v((2 * TOK, WID), BF16), v((2 * TOK, WID), BF16),
        v((8, BLK, WID), F32), v((WID, WID), BF16), v((WID, WID), BF16),
        v((4, TOK, WID), F32), v((4, TOK, WID), BF16), v((4, TOK, WID), BF16),
        v((TOK, WID), F32), v((TOK, WID), F32), v((2 * TOK, WID), BF16), v((2 * TOK, WID), BF16),
        v((8, TOK, BLK), F32), v((4, TOK, BLK), F32), v((8, TOK, BLK), F32),
        v((4, BLK, 2 * TOK), BF16), v((4, BLK, 2 * TOK), BF16), v((4, BLK, 2 * TOK), BF16), v((4, BLK, 2 * TOK), BF16),
        *[v((8, TOK, BLK), F32)] * 5,
        v((TOK, WID), BF16), v((TOK, WID), BF16), v((4, TOK, BLK), F32), v((4, TOK, BLK), F32),
        v((2, 6, BLK, HALF), F32), v((2, 6, BLK, HALF), F32), v((2, 2, BLK, HALF), F32),
        v((PARTS, 6, ROWS // 2, 2 * BLK), F32), v((PARTS, 6, ROWS // 2, 2 * BLK), F32), v((PARTS, ROWS, 2 * BLK), F32),
        v((PARTS, ROWS, BLK), F32), v((PARTS, ROWS, BLK), F32),
        dma((22,)), dma((11,)), dma((11,)), dma((2, len(CHUNKS))), dma((2, len(CHUNKS))),
        dma((2, 6)), dma((2, 6)), dma((PARTS, 6)), dma((PARTS, 6)), dma((PARTS,)), dma((PARTS,)),
        *[pltpu.SemaphoreType.REGULAR] * 3,
    ]
    results = pl.pallas_call(
        kernel,
        out_shape=(v((TOK, BLK), F32), v((WID, BLK), F32), v((BLK, WID), F32)),
        in_specs=[pl.BlockSpec(memory_space=pl.ANY)] * 5,
        out_specs=[pl.BlockSpec(memory_space=pltpu.VMEM)] * 3,
        scratch_shapes=scratch,
        compiler_params=pltpu.CompilerParams(collective_id=0, has_side_effects=True, vmem_limit_bytes=60 << 20),
        cost_estimate=pl.CostEstimate(flops=6_442_450_944, bytes_accessed=13 << 20, transcendentals=1 << 19),
        name="mlp_backward",
    )(inputs, pre_act, w_in, w_out, grad_out)
    return pl.pallas_call(
        write_out,
        out_shape=[jax.ShapeDtypeStruct(r.shape, F32) for r in results],
        in_specs=[pl.BlockSpec(memory_space=pl.ANY)] * 3,
        out_specs=[pl.BlockSpec(memory_space=pl.ANY)] * 3,
        scratch_shapes=[dma((3,))],
        compiler_params=pltpu.CompilerParams(vmem_limit_bytes=2 << 20),
        name="write_out",
    )(*results)


def solution(mesh):
    in_specs = (P("gz", "gx"), P("gz", "gy"), P("gx", "gy"), P("gy", "gx"), P("gz", "gx"))
    out_specs = (P("gz", ("gx", "gy")), P("gx", ("gy", "gz")), P(("gy", "gz"), "gx"))
    return jax.shard_map(
        per_device, mesh=mesh, in_specs=in_specs, out_specs=out_specs, check_vma=False
    )
```

```python
import functools

import jax
import jax.numpy as jnp
from jax import lax
from jax.experimental import pallas as pl
from jax.experimental.pallas import tpu as pltpu
from jax.sharding import PartitionSpec as P

MESH = pl.DeviceIdType.MESH
F32 = jnp.float32
BF16 = jnp.bfloat16
sqrt_two_pi = 0.7978845608028654
cubic_coef = 0.044715

TOK = 256
WID = 1024
BLK = 128
HALF = 512
PARTS = 2
ROWS = TOK // PARTS
SUB = 64
CHUNKS = [(k, e, r) for t in range(PARTS) for k in range(4) for e in range(2) for r in range(t * ROWS, (t + 1) * ROWS, SUB)]
LAG = 5
AHEAD = 4
FLIGHT = 6

NN = (((1,), (0,)), ((), ()))
NT = (((1,), (1,)), ((), ()))


def split(value):
    high = value.astype(BF16)
    return high, (value - high.astype(F32)).astype(BF16)


def dot3(left, right, dims):
    (lh, ll), (rh, rl) = left, right
    d = lambda a, b: lax.dot_general(a, b, dims, preferred_element_type=F32)
    return d(lh, rh) + (d(lh, rl) + d(ll, rh))


def tangent_of(v):
    return jnp.tanh(sqrt_two_pi * (v + cubic_coef * v * v * v))


def gelu_value(v, t):
    return 0.5 * v * (1.0 + t)


def gelu_slope(v, t):
    return 0.5 * (1.0 + t) + 0.5 * v * (1.0 - t * t) * sqrt_two_pi * (1.0 + 3.0 * cubic_coef * v * v)


def kernel(
    x_in, p_in, wi_in, wo_in, g_in, gi_v, gwi_v, gwo_v,
    g_v, gs_v, g_h, g_l, wo_v, wo_h, wo_l, wi_v, wi_h, wi_l, x_v, xs_v, x_h, x_l,
    p_v, ps_v, der_v, a_h, a_l, h_h, h_l, own_z, rp, rs, sp, ss, hid_h, hid_l, hsend, hs_v,
    xsend, xrecv, xown, ysend, yrecv, yown, hsnd, hrcv,
    lsem, csend, crecv, zsend, zrecv, xss, xrs, yss, yrs, vss, vrs, core_in, z_in, v_in,
):
    gx, gy, gz = lax.axis_index("gx"), lax.axis_index("gy"), lax.axis_index("gz")
    y, zh, x, c = gy // 2, gy % 2, gz // 2, gz % 2
    xp, xm, xo = (x + 1) % 4, (x + 3) % 4, (x + 2) % 4
    yp, ym, yo = (y + 1) % 4, (y + 3) % 4, (y + 2) % 4
    owners = (xo, xp, xm, x)
    yowners = (yo, yp, ym, y)
    sibling = (gx, gy, x * 2 + 1 - c)
    x_next, x_prev = (gx, gy, xp * 2 + c), (gx, gy, xm * 2 + c)
    y_next, y_prev = (gx, yp * 2 + zh, gz), (gx, ym * 2 + zh, gz)
    partner = (gx, y * 2 + 1 - zh, gz)
    z_next, z_prev = ((gx + 1) % 4, gy, gz), ((gx + 3) % 4, gy, gz)

    def block(k, e):
        return 2 * owners[k] + (c if e else 1 - c)

    def cols(k, e):
        return pl.ds(pl.multiple_of(block(k, e) * BLK, BLK), BLK)

    def load(src, dst, n):
        return pltpu.make_async_copy(src, dst, lsem.at[n])

    l_g = load(g_in, g_v, 0)
    l_wo = [[load(wo_in.at[cols(k, e), :], wo_v.at[2 * k + e], 1 + 2 * k + e) for e in range(2)] for k in range(4)]
    l_p = [[load(p_in.at[:, cols(k, e)], p_v.at[2 * k + e], 9 + 2 * k + e) for e in range(2)] for k in range(4)]
    l_x = load(x_in, x_v, 17)
    l_wi = [
        load(wi_in.at[pl.ds(pl.multiple_of(yowners[n] * TOK, TOK), TOK), :], wi_v.at[n], 18 + n) for n in range(4)
    ]
    l_g.start()
    for e in range(2):
        l_wo[0][e].start()
    for e in range(2):
        l_p[0][e].start()

    barrier = pltpu.get_barrier_semaphore()
    def tell(sem, who):
        pl.semaphore_signal(sem, inc=1, device_id=who, device_id_type=MESH)

    for who in (x_next, x_prev, y_next, y_prev):
        tell(barrier, who)
    pl.when(c == 0)(lambda: tell(barrier, sibling))
    pl.when(gx < 3)(lambda: tell(barrier, z_next))
    pl.when(zh == 0)(lambda: tell(barrier, partner))
    pl.semaphore_wait(barrier, 4 + c + jnp.where(gx > 0, 1, 0) + zh)
    pl.when(c == 1)(lambda: tell(core_in, sibling))
    pl.when(gx > 0)(lambda: tell(z_in, z_prev))
    pl.when(zh == 1)(lambda: tell(v_in, partner))

    def remote(src, dst, s_sem, r_sem, who):
        return pltpu.make_async_remote_copy(
            src_ref=src, dst_ref=dst, send_sem=s_sem, recv_sem=r_sem, device_id=who, device_id_type=MESH
        )

    c_p = [remote(p_in.at[:, cols(k, 0)], ps_v.at[k], csend.at[k], crecv.at[k], sibling) for k in range(4)]
    c_g = [
        remote(g_in.at[:, pl.ds(h * HALF, HALF)], gs_v.at[h], csend.at[4 + h], crecv.at[4 + h], sibling)
        for h in range(2)
    ]
    c_x = remote(x_in, xs_v, csend.at[6], crecv.at[6], sibling)
    c_h = [remote(hsend.at[k], hs_v.at[k], csend.at[7 + k], crecv.at[7 + k], sibling) for k in range(4)]
    def greet_sibling():
        c_p[0].start()
        c_g[0].start()
        c_g[1].start()
        for k in range(1, 4):
            c_p[k].start()

    @pl.when(gx == 0)
    def _():
        rp[...] = jnp.zeros_like(rp)

    @pl.when(gx == 3)
    def _():
        rs[...] = jnp.zeros_like(rs)

    def where(i):
        k, e, r = CHUNKS[i]
        return (2 * k + e, pl.ds(r, SUB))

    def z_copy(src, dst, way, i):
        b, rows = where(i)
        return remote(
            src.at[b, rows], dst.at[b, rows], zsend.at[way, i], zrecv.at[way, i], z_next if way == 0 else z_prev
        )

    def right(i, src=None):
        return z_copy(sp if src is None else src, rp, 0, i)

    def left(i, src=None):
        return z_copy(ss if src is None else src, rs, 1, i)

    def z_own(send, i):
        if i < n_chunks:
            if i >= FLIGHT:
                send(i - FLIGHT).wait_send()
            send(i, own_z).start()

    def forward(send, total, came, i):
        if 0 <= i < n_chunks:
            b, rows = where(i)
            send(i).wait_recv()
            total[b, rows] = own_z[b, rows] + came[b, rows]
            send(i).start()

    def z_begin():
        @pl.when(gx == 0)
        def _():
            pl.semaphore_wait(z_in, 1)
            for i in range(AHEAD):
                z_own(right, i)

        @pl.when(gx == 3)
        def _():
            for i in range(AHEAD):
                z_own(left, i)

        @pl.when((gx == 1) | (gx == 2))
        def _():
            pl.semaphore_wait(z_in, 1)

    n_chunks = len(CHUNKS)

    def z_group(j):
        pair = (2 * j, 2 * j + 1)
        last = [i - 2 * LAG for i in pair if 0 <= i - 2 * LAG < n_chunks]

        @pl.when(gx == 0)
        def _():
            for i in pair:
                z_own(right, i + AHEAD)
            for i in last:
                left(i).wait_recv()

        @pl.when(gx == 1)
        def _():
            for i in pair:
                forward(right, sp, rp, i)
                forward(left, ss, rs, i - LAG)

        @pl.when(gx == 2)
        def _():
            for i in pair:
                forward(left, ss, rs, i)
                forward(right, sp, rp, i - LAG)

        @pl.when(gx == 3)
        def _():
            for i in pair:
                z_own(left, i + AHEAD)
            for i in last:
                right(i).wait_recv()

        if last:
            k, e, r = CHUNKS[last[0]]
            b, rows = 2 * k + e, pl.ds(r, 2 * SUB)
            hidden = (own_z[b, rows] + rp[b, rows] + rs[b, rows]) * der_v[b, rows]
            high, low = split(hidden)
            hid_h[rows, cols(k, e)] = high
            hid_l[rows, cols(k, e)] = low
            if e == 0:
                hsend[k, rows] = hidden
                if r + 2 * SUB == TOK:
                    c_h[k].start()
            else:
                high, low = split(hidden.T)
                h_h[k, :, rows] = high
                h_l[k, :, rows] = low

    def partial(k):
        for e in range(2):
            l_wo[k][e].wait()
            b = 2 * k + e
            wo_h[pl.ds(b * BLK, BLK), :], wo_l[pl.ds(b * BLK, BLK), :] = split(wo_v[b])
        rows = pl.ds(2 * k * BLK, 2 * BLK)
        value = dot3((g_h[:TOK, :], g_l[:TOK, :]), (wo_h[rows, :], wo_l[rows, :]), NT)
        own_z[2 * k] = value[:, :BLK]
        own_z[2 * k + 1] = value[:, BLK:]

    def gelu(k):
        for e in range(2):
            l_p[k][e].wait()
            v = p_v[2 * k + e]
            t = tangent_of(v)
            der_v[2 * k + e] = gelu_slope(v, t)
            if e == 1:
                a_h[k, :, :TOK], a_l[k, :, :TOK] = split(gelu_value(v, t).T)
        if k > 0:
            gelu_sibling(k)

    def gelu_sibling(k):
        c_p[k].wait_recv()
        v = ps_v[k]
        a_h[k, :, TOK:], a_l[k, :, TOK:] = split(gelu_value(v, tangent_of(v)).T)

    def x_copy(g, m):
        return remote(xsend.at[g, m], xrecv.at[g, m], xss.at[g, m], xrs.at[g, m], x_next if m % 2 == 0 else x_prev)

    def weight(g, k, h):
        th, tl, vh, vl = (a_h, a_l, g_h, g_l) if g == 0 else (h_h, h_l, x_h, x_l)
        half = pl.ds(h * HALF, HALF)
        return dot3((th[k], tl[k]), (vh[:, half], vl[:, half]), NN)

    def x_send(g, m, k, h):
        xsend[g, m] = weight(g, k, h)
        x_copy(g, m).start()

    def x_first(g):
        x_send(g, 1, 0, 0)
        x_send(g, 0, 0, 1)

    def x_second(g):
        x_send(g, 2, 1, 0)
        x_send(g, 3, 2, 1)

    def x_third_local(g):
        xsend[g, 4] = weight(g, 1, 1)
        xsend[g, 5] = weight(g, 2, 0)

    def x_third(g):
        for m in (4, 5):
            x_copy(g, m - 4).wait_recv()
            xsend[g, m] = xsend[g, m] + xrecv[g, m - 4]
            x_copy(g, m).start()

    def x_own(g):
        xown[g, 0] = weight(g, 3, 0)
        xown[g, 1] = weight(g, 3, 1)

    def x_final(g):
        for h, ms in ((0, (2, 5)), (1, (3, 4))):
            for m in ms:
                x_copy(g, m).wait_recv()
            total = xown[g, h] + xrecv[g, ms[0]] + xrecv[g, ms[1]]
            half = pl.ds(h * HALF, HALF)
            if g == 0:
                gwo_v[:, half] = total
            else:
                gwi_v[half, :] = total.T

    def x_begin():
        gelu_sibling(0)
        for h in range(2):
            c_g[h].wait_recv()
            half = pl.ds(h * HALF, HALF)
            g_h[TOK:, half], g_l[TOK:, half] = split(gs_v[h])
        x_first(0)

    def hidden_sibling(k):
        c_h[k].wait_recv()
        h_h[k, :, TOK:], h_l[k, :, TOK:] = split(hs_v[k].T)

    def split_inputs():
        l_x.wait()
        x_h[:TOK, :], x_l[:TOK, :] = split(x_v[...])
        c_x.wait_recv()
        x_h[TOK:, :], x_l[TOK:, :] = split(xs_v[...])

    def split_w_in(n):
        l_wi[n].wait()
        wi_h[n], wi_l[n] = split(wi_v[n])

    QR = ROWS // 2

    def y_copy(t, m):
        return remote(ysend.at[t, m], yrecv.at[t, m], yss.at[t, m], yrs.at[t, m], y_next if m % 2 == 0 else y_prev)

    def y_block(t, n):
        rows = pl.ds(t * ROWS, ROWS)
        return dot3((hid_h[rows, :], hid_l[rows, :]), (wi_h[n], wi_l[n]), NT)

    def y_send(t, m, value):
        ysend[t, m] = value
        y_copy(t, m).start()

    def y_first(t):
        v = y_block(t, 0)
        y_send(t, 1, v[:QR])
        y_send(t, 0, v[QR:])

    def y_second(t):
        v = y_block(t, 1)
        y_send(t, 2, v[:QR])
        ysend[t, 4] = v[QR:]
        v = y_block(t, 2)
        y_send(t, 3, v[QR:])
        ysend[t, 5] = v[:QR]

    def y_third(t):
        for m in (4, 5):
            y_copy(t, m - 4).wait_recv()
            ysend[t, m] = ysend[t, m] + yrecv[t, m - 4]
            y_copy(t, m).start()

    def y_own(t):
        yown[t] = y_block(t, 3)

    def v_copy(t):
        return remote(hsnd.at[t], hrcv.at[t], vss.at[t], vrs.at[t], partner)

    def y_final(t):
        for h, ms in ((0, (2, 5)), (1, (3, 4))):
            for m in ms:
                y_copy(t, m).wait_recv()
            rows = pl.ds(h * QR, QR)
            total = yown[t, rows] + yrecv[t, ms[0]] + yrecv[t, ms[1]]
            low, high = total[:, :BLK], total[:, BLK:]
            hsnd[t, rows] = jnp.where(zh == 0, high, low)
            gi_v[pl.ds(t * ROWS + h * QR, QR), :] = jnp.where(zh == 0, low, high)
        if t == 0:
            pl.when(zh == 0)(lambda: pl.semaphore_wait(v_in, 1))
        v_copy(t).start()

    def v_final(t):
        v_copy(t).wait_recv()
        rows = pl.ds(t * ROWS, ROWS)
        gi_v[rows, :] = gi_v[rows, :] + hrcv[t]

    pl.when(c == 1)(greet_sibling)
    l_g.wait()
    for k in range(1, 4):
        for e in range(2):
            l_wo[k][e].start()
    g_h[:TOK, :], g_l[:TOK, :] = split(g_v[...])
    partial(0)
    for k in range(1, 4):
        for e in range(2):
            l_p[k][e].start()
    l_x.start()
    for n in range(4):
        l_wi[n].start()
    z_begin()

    @pl.when(c == 0)
    def _():
        pl.semaphore_wait(core_in, 1)
        greet_sibling()

    gelu(0)
    pl.when(c == 1)(x_begin)
    partial(1)
    z_group(0)
    pl.when(c == 0)(x_begin)
    z_group(1)
    partial(2)
    z_group(2)
    c_x.start()
    gelu(1)
    z_group(3)
    partial(3)
    z_group(4)
    gelu(2)
    x_second(0)
    z_group(5)
    x_third_local(0)
    z_group(6)
    gelu(3)
    z_group(7)
    x_third(0)
    z_group(8)
    split_w_in(0)
    z_group(9)
    split_w_in(1)
    z_group(10)
    split_w_in(2)
    z_group(11)
    split_w_in(3)
    z_group(12)
    y_first(0)
    z_group(13)
    split_inputs()
    z_group(14)
    y_second(0)
    z_group(15)
    hidden_sibling(0)
    x_first(1)
    z_group(16)
    y_third(0)
    z_group(17)
    z_group(18)
    hidden_sibling(1)
    hidden_sibling(2)
    z_group(19)
    x_second(1)
    z_group(20)
    y_first(1)
    y_second(1)
    x_third_local(1)
    y_own(0)
    y_final(0)
    x_third(1)
    y_third(1)
    y_own(1)
    x_own(0)
    x_final(0)
    hidden_sibling(3)
    x_own(1)
    v_final(0)
    y_final(1)
    x_final(1)
    v_final(1)

    def all_left(sends, first=0):
        for i in range(first, n_chunks):
            for send in sends:
                send(i).wait_send()

    pl.when(gx == 0)(lambda: all_left((right,), n_chunks - FLIGHT))
    pl.when((gx == 1) | (gx == 2))(lambda: all_left((right, left)))
    pl.when(gx == 3)(lambda: all_left((left,), n_chunks - FLIGHT))
    for copy in (*c_p, *c_g, c_x, *c_h):
        copy.wait_send()
    for m in range(6):
        for g in range(2):
            x_copy(g, m).wait_send()
        for t in range(PARTS):
            y_copy(t, m).wait_send()
    for t in range(PARTS):
        v_copy(t).wait_send()


def write_out(*refs):
    copies = [pltpu.make_async_copy(refs[n], refs[3 + n], refs[6].at[n]) for n in range(3)]
    for copy in copies:
        copy.start()
    for copy in copies:
        copy.wait()


def per_device(inputs, pre_act, w_in, w_out, grad_out):
    v = pltpu.VMEM
    dma = pltpu.SemaphoreType.DMA
    scratch = [
        v((TOK, WID), F32), v((2, TOK, HALF), F32), v((2 * TOK, WID), BF16), v((2 * TOK, WID), BF16),
        v((8, BLK, WID), F32), v((WID, WID), BF16), v((WID, WID), BF16),
        v((4, TOK, WID), F32), v((4, TOK, WID), BF16), v((4, TOK, WID), BF16),
        v((TOK, WID), F32), v((TOK, WID), F32), v((2 * TOK, WID), BF16), v((2 * TOK, WID), BF16),
        v((8, TOK, BLK), F32), v((4, TOK, BLK), F32), v((8, TOK, BLK), F32),
        v((4, BLK, 2 * TOK), BF16), v((4, BLK, 2 * TOK), BF16), v((4, BLK, 2 * TOK), BF16), v((4, BLK, 2 * TOK), BF16),
        *[v((8, TOK, BLK), F32)] * 5,
        v((TOK, WID), BF16), v((TOK, WID), BF16), v((4, TOK, BLK), F32), v((4, TOK, BLK), F32),
        v((2, 6, BLK, HALF), F32), v((2, 6, BLK, HALF), F32), v((2, 2, BLK, HALF), F32),
        v((PARTS, 6, ROWS // 2, 2 * BLK), F32), v((PARTS, 6, ROWS // 2, 2 * BLK), F32), v((PARTS, ROWS, 2 * BLK), F32),
        v((PARTS, ROWS, BLK), F32), v((PARTS, ROWS, BLK), F32),
        dma((22,)), dma((11,)), dma((11,)), dma((2, len(CHUNKS))), dma((2, len(CHUNKS))),
        dma((2, 6)), dma((2, 6)), dma((PARTS, 6)), dma((PARTS, 6)), dma((PARTS,)), dma((PARTS,)),
        *[pltpu.SemaphoreType.REGULAR] * 3,
    ]
    results = pl.pallas_call(
        kernel,
        out_shape=(v((TOK, BLK), F32), v((WID, BLK), F32), v((BLK, WID), F32)),
        in_specs=[pl.BlockSpec(memory_space=pl.ANY)] * 5,
        out_specs=[pl.BlockSpec(memory_space=pltpu.VMEM)] * 3,
        scratch_shapes=scratch,
        compiler_params=pltpu.CompilerParams(collective_id=0, has_side_effects=True, vmem_limit_bytes=60 << 20),
        cost_estimate=pl.CostEstimate(flops=6_442_450_944, bytes_accessed=13 << 20, transcendentals=1 << 19),
        name="mlp_backward",
    )(inputs, pre_act, w_in, w_out, grad_out)
    return pl.pallas_call(
        write_out,
        out_shape=[jax.ShapeDtypeStruct(r.shape, F32) for r in results],
        in_specs=[pl.BlockSpec(memory_space=pl.ANY)] * 3,
        out_specs=[pl.BlockSpec(memory_space=pl.ANY)] * 3,
        scratch_shapes=[dma((3,))],
        compiler_params=pltpu.CompilerParams(vmem_limit_bytes=2 << 20),
        name="write_out",
    )(*results)


def solution(mesh):
    in_specs = (P("gz", "gx"), P("gz", "gy"), P("gx", "gy"), P("gy", "gx"), P("gz", "gx"))
    out_specs = (P("gz", ("gx", "gy")), P("gx", ("gy", "gz")), P(("gy", "gz"), "gx"))
    return jax.shard_map(
        per_device, mesh=mesh, in_specs=in_specs, out_specs=out_specs, check_vma=False
    )
```

```python
import functools

import jax
import jax.numpy as jnp
from jax import lax
from jax.experimental import pallas as pl
from jax.experimental.pallas import tpu as pltpu
from jax.sharding import PartitionSpec as P

MESH = pl.DeviceIdType.MESH
F32 = jnp.float32
BF16 = jnp.bfloat16
sqrt_two_pi = 0.7978845608028654
cubic_coef = 0.044715

TOK = 256
WID = 1024
BLK = 128
HALF = 512
PARTS = 2
ROWS = TOK // PARTS
SUB = 64
CHUNKS = [(k, e, r) for t in range(PARTS) for k in range(4) for e in range(2) for r in range(t * ROWS, (t + 1) * ROWS, SUB)]
LAG = 5
AHEAD = 4
FLIGHT = 6

NN = (((1,), (0,)), ((), ()))
NT = (((1,), (1,)), ((), ()))


def split(value):
    high = value.astype(BF16)
    return high, (value - high.astype(F32)).astype(BF16)


def dot3(left, right, dims):
    (lh, ll), (rh, rl) = left, right
    d = lambda a, b: lax.dot_general(a, b, dims, preferred_element_type=F32)
    return d(lh, rh) + (d(lh, rl) + d(ll, rh))


def tangent_of(v):
    return jnp.tanh(sqrt_two_pi * (v + cubic_coef * v * v * v))


def gelu_value(v, t):
    return 0.5 * v * (1.0 + t)


def gelu_slope(v, t):
    return 0.5 * (1.0 + t) + 0.5 * v * (1.0 - t * t) * sqrt_two_pi * (1.0 + 3.0 * cubic_coef * v * v)


def kernel(
    x_in, p_in, wi_in, wo_in, g_in, gi_v, gwi_v, gwo_v,
    g_v, gs_v, g_h, g_l, wo_v, wo_h, wo_l, wi_v, wi_h, wi_l, x_v, xs_v, x_h, x_l,
    p_v, ps_v, der_v, a_h, a_l, h_h, h_l, own_z, rp, rs, sp, ss, hid_h, hid_l, hsend, hs_v,
    xsend, xrecv, xown, ysend, yrecv, yown, hsnd, hrcv,
    lsem, csend, crecv, zsend, zrecv, xss, xrs, yss, yrs, vss, vrs, core_in, z_in, v_in,
):
    gx, gy, gz = lax.axis_index("gx"), lax.axis_index("gy"), lax.axis_index("gz")
    y, zh, x, c = gy // 2, gy % 2, gz // 2, gz % 2
    xp, xm, xo = (x + 1) % 4, (x + 3) % 4, (x + 2) % 4
    yp, ym, yo = (y + 1) % 4, (y + 3) % 4, (y + 2) % 4
    owners = (xo, xp, xm, x)
    yowners = (yo, yp, ym, y)
    sibling = (gx, gy, x * 2 + 1 - c)
    x_next, x_prev = (gx, gy, xp * 2 + c), (gx, gy, xm * 2 + c)
    y_next, y_prev = (gx, yp * 2 + zh, gz), (gx, ym * 2 + zh, gz)
    partner = (gx, y * 2 + 1 - zh, gz)
    z_next, z_prev = ((gx + 1) % 4, gy, gz), ((gx + 3) % 4, gy, gz)

    def block(k, e):
        return 2 * owners[k] + (c if e else 1 - c)

    def cols(k, e):
        return pl.ds(pl.multiple_of(block(k, e) * BLK, BLK), BLK)

    def load(src, dst, n):
        return pltpu.make_async_copy(src, dst, lsem.at[n])

    l_g = load(g_in, g_v, 0)
    l_wo = [[load(wo_in.at[cols(k, e), :], wo_v.at[2 * k + e], 1 + 2 * k + e) for e in range(2)] for k in range(4)]
    l_p = [[load(p_in.at[:, cols(k, e)], p_v.at[2 * k + e], 9 + 2 * k + e) for e in range(2)] for k in range(4)]
    l_x = load(x_in, x_v, 17)
    l_wi = [
        load(wi_in.at[pl.ds(pl.multiple_of(yowners[n] * TOK, TOK), TOK), :], wi_v.at[n], 18 + n) for n in range(4)
    ]
    l_g.start()
    for e in range(2):
        l_wo[0][e].start()
    for e in range(2):
        l_p[0][e].start()

    barrier = pltpu.get_barrier_semaphore()
    def tell(sem, who):
        pl.semaphore_signal(sem, inc=1, device_id=who, device_id_type=MESH)

    for who in (x_next, x_prev, y_next, y_prev):
        tell(barrier, who)
    pl.when(c == 0)(lambda: tell(barrier, sibling))
    pl.when(gx < 3)(lambda: tell(barrier, z_next))
    pl.when(zh == 0)(lambda: tell(barrier, partner))
    pl.semaphore_wait(barrier, 4 + c + jnp.where(gx > 0, 1, 0) + zh)
    pl.when(c == 1)(lambda: tell(core_in, sibling))
    pl.when(gx > 0)(lambda: tell(z_in, z_prev))
    pl.when(zh == 1)(lambda: tell(v_in, partner))

    def remote(src, dst, s_sem, r_sem, who):
        return pltpu.make_async_remote_copy(
            src_ref=src, dst_ref=dst, send_sem=s_sem, recv_sem=r_sem, device_id=who, device_id_type=MESH
        )

    c_p = [remote(p_in.at[:, cols(k, 0)], ps_v.at[k], csend.at[k], crecv.at[k], sibling) for k in range(4)]
    c_g = [
        remote(g_in.at[:, pl.ds(h * HALF, HALF)], gs_v.at[h], csend.at[4 + h], crecv.at[4 + h], sibling)
        for h in range(2)
    ]
    c_x = remote(x_in, xs_v, csend.at[6], crecv.at[6], sibling)
    c_h = [remote(hsend.at[k], hs_v.at[k], csend.at[7 + k], crecv.at[7 + k], sibling) for k in range(4)]
    def greet_sibling():
        c_p[0].start()
        c_g[0].start()
        c_g[1].start()
        for k in range(1, 4):
            c_p[k].start()

    @pl.when(gx == 0)
    def _():
        rp[...] = jnp.zeros_like(rp)

    @pl.when(gx == 3)
    def _():
        rs[...] = jnp.zeros_like(rs)

    def where(i):
        k, e, r = CHUNKS[i]
        return (2 * k + e, pl.ds(r, SUB))

    def z_copy(src, dst, way, i):
        b, rows = where(i)
        return remote(
            src.at[b, rows], dst.at[b, rows], zsend.at[way, i], zrecv.at[way, i], z_next if way == 0 else z_prev
        )

    def right(i, src=None):
        return z_copy(sp if src is None else src, rp, 0, i)

    def left(i, src=None):
        return z_copy(ss if src is None else src, rs, 1, i)

    def z_own(send, i):
        if i < n_chunks:
            if i >= FLIGHT:
                send(i - FLIGHT).wait_send()
            send(i, own_z).start()

    def forward(send, total, came, i):
        if 0 <= i < n_chunks:
            b, rows = where(i)
            send(i).wait_recv()
            total[b, rows] = own_z[b, rows] + came[b, rows]
            send(i).start()

    def z_begin(first, last):
        @pl.when(gx == 0)
        def _():
            if first == 0:
                pl.semaphore_wait(z_in, 1)
            for i in range(first, last):
                z_own(right, i)

        @pl.when(gx == 3)
        def _():
            for i in range(first, last):
                z_own(left, i)

        if first == 0:

            @pl.when((gx == 1) | (gx == 2))
            def _():
                pl.semaphore_wait(z_in, 1)

    n_chunks = len(CHUNKS)

    def z_group(j):
        pair = (2 * j, 2 * j + 1)
        last = [i - 2 * LAG for i in pair if 0 <= i - 2 * LAG < n_chunks]

        @pl.when(gx == 0)
        def _():
            for i in pair:
                z_own(right, i + AHEAD)
            for i in last:
                left(i).wait_recv()

        @pl.when(gx == 1)
        def _():
            for i in pair:
                forward(right, sp, rp, i)
                forward(left, ss, rs, i - LAG)

        @pl.when(gx == 2)
        def _():
            for i in pair:
                forward(left, ss, rs, i)
                forward(right, sp, rp, i - LAG)

        @pl.when(gx == 3)
        def _():
            for i in pair:
                z_own(left, i + AHEAD)
            for i in last:
                right(i).wait_recv()

        if last:
            k, e, r = CHUNKS[last[0]]
            b, rows = 2 * k + e, pl.ds(r, 2 * SUB)
            hidden = (own_z[b, rows] + rp[b, rows] + rs[b, rows]) * der_v[b, rows]
            high, low = split(hidden)
            hid_h[rows, cols(k, e)] = high
            hid_l[rows, cols(k, e)] = low
            if e == 0:
                hsend[k, rows] = hidden
                if r + 2 * SUB == TOK:
                    c_h[k].start()
            else:
                high, low = split(hidden.T)
                h_h[k, :, rows] = high
                h_l[k, :, rows] = low

    def partial(k):
        for e in range(2):
            l_wo[k][e].wait()
            b = 2 * k + e
            wo_h[pl.ds(b * BLK, BLK), :], wo_l[pl.ds(b * BLK, BLK), :] = split(wo_v[b])
        rows = pl.ds(2 * k * BLK, 2 * BLK)
        value = dot3((g_h[:TOK, :], g_l[:TOK, :]), (wo_h[rows, :], wo_l[rows, :]), NT)
        own_z[2 * k] = value[:, :BLK]
        own_z[2 * k + 1] = value[:, BLK:]

    def partial_block(k, e):
        l_wo[k][e].wait()
        b = 2 * k + e
        value = dot3((g_h[:TOK, :], g_l[:TOK, :]), split(wo_v[b]), NT)
        own_z[b] = value

    def gelu(k):
        for e in range(2):
            l_p[k][e].wait()
            v = p_v[2 * k + e]
            t = tangent_of(v)
            der_v[2 * k + e] = gelu_slope(v, t)
            if e == 1:
                a_h[k, :, :TOK], a_l[k, :, :TOK] = split(gelu_value(v, t).T)
        if k > 0:
            gelu_sibling(k)

    def gelu_sibling(k):
        c_p[k].wait_recv()
        v = ps_v[k]
        a_h[k, :, TOK:], a_l[k, :, TOK:] = split(gelu_value(v, tangent_of(v)).T)

    def x_copy(g, m):
        return remote(xsend.at[g, m], xrecv.at[g, m], xss.at[g, m], xrs.at[g, m], x_next if m % 2 == 0 else x_prev)

    def weight(g, k, h):
        th, tl, vh, vl = (a_h, a_l, g_h, g_l) if g == 0 else (h_h, h_l, x_h, x_l)
        half = pl.ds(h * HALF, HALF)
        return dot3((th[k], tl[k]), (vh[:, half], vl[:, half]), NN)

    def x_send(g, m, k, h):
        xsend[g, m] = weight(g, k, h)
        x_copy(g, m).start()

    def x_first(g):
        x_send(g, 1, 0, 0)
        x_send(g, 0, 0, 1)

    def x_second(g):
        x_send(g, 2, 1, 0)
        x_send(g, 3, 2, 1)

    def x_third_local(g):
        xsend[g, 4] = weight(g, 1, 1)
        xsend[g, 5] = weight(g, 2, 0)

    def x_third(g):
        for m in (4, 5):
            x_copy(g, m - 4).wait_recv()
            xsend[g, m] = xsend[g, m] + xrecv[g, m - 4]
            x_copy(g, m).start()

    def x_own(g):
        xown[g, 0] = weight(g, 3, 0)
        xown[g, 1] = weight(g, 3, 1)

    def x_final(g):
        for h, ms in ((0, (2, 5)), (1, (3, 4))):
            for m in ms:
                x_copy(g, m).wait_recv()
            total = xown[g, h] + xrecv[g, ms[0]] + xrecv[g, ms[1]]
            half = pl.ds(h * HALF, HALF)
            if g == 0:
                gwo_v[:, half] = total
            else:
                gwi_v[half, :] = total.T

    def x_begin():
        gelu_sibling(0)
        for h in range(2):
            c_g[h].wait_recv()
            half = pl.ds(h * HALF, HALF)
            g_h[TOK:, half], g_l[TOK:, half] = split(gs_v[h])
        x_first(0)

    def hidden_sibling(k):
        c_h[k].wait_recv()
        h_h[k, :, TOK:], h_l[k, :, TOK:] = split(hs_v[k].T)

    def split_inputs():
        l_x.wait()
        x_h[:TOK, :], x_l[:TOK, :] = split(x_v[...])
        c_x.wait_recv()
        x_h[TOK:, :], x_l[TOK:, :] = split(xs_v[...])

    def split_w_in(n):
        l_wi[n].wait()
        wi_h[n], wi_l[n] = split(wi_v[n])

    QR = ROWS // 2

    def y_copy(t, m):
        return remote(ysend.at[t, m], yrecv.at[t, m], yss.at[t, m], yrs.at[t, m], y_next if m % 2 == 0 else y_prev)

    def y_block(t, n):
        rows = pl.ds(t * ROWS, ROWS)
        return dot3((hid_h[rows, :], hid_l[rows, :]), (wi_h[n], wi_l[n]), NT)

    def y_send(t, m, value):
        ysend[t, m] = value
        y_copy(t, m).start()

    def y_first(t):
        v = y_block(t, 0)
        y_send(t, 1, v[:QR])
        y_send(t, 0, v[QR:])

    def y_second(t):
        v = y_block(t, 1)
        y_send(t, 2, v[:QR])
        ysend[t, 4] = v[QR:]
        v = y_block(t, 2)
        y_send(t, 3, v[QR:])
        ysend[t, 5] = v[:QR]

    def y_third(t):
        for m in (4, 5):
            y_copy(t, m - 4).wait_recv()
            ysend[t, m] = ysend[t, m] + yrecv[t, m - 4]
            y_copy(t, m).start()

    def y_own(t):
        yown[t] = y_block(t, 3)

    def v_copy(t):
        return remote(hsnd.at[t], hrcv.at[t], vss.at[t], vrs.at[t], partner)

    def y_final(t):
        for h, ms in ((0, (2, 5)), (1, (3, 4))):
            for m in ms:
                y_copy(t, m).wait_recv()
            rows = pl.ds(h * QR, QR)
            total = yown[t, rows] + yrecv[t, ms[0]] + yrecv[t, ms[1]]
            low, high = total[:, :BLK], total[:, BLK:]
            hsnd[t, rows] = jnp.where(zh == 0, high, low)
            gi_v[pl.ds(t * ROWS + h * QR, QR), :] = jnp.where(zh == 0, low, high)
        if t == 0:
            pl.when(zh == 0)(lambda: pl.semaphore_wait(v_in, 1))
        v_copy(t).start()

    def v_final(t):
        v_copy(t).wait_recv()
        rows = pl.ds(t * ROWS, ROWS)
        gi_v[rows, :] = gi_v[rows, :] + hrcv[t]

    pl.when(c == 1)(greet_sibling)
    l_g.wait()
    for k in range(1, 4):
        for e in range(2):
            l_wo[k][e].start()
    g_h[:TOK, :], g_l[:TOK, :] = split(g_v[...])
    partial_block(0, 0)
    z_begin(0, AHEAD // 2)
    partial_block(0, 1)
    for k in range(1, 4):
        for e in range(2):
            l_p[k][e].start()
    l_x.start()
    for n in range(4):
        l_wi[n].start()
    z_begin(AHEAD // 2, AHEAD)

    @pl.when(c == 0)
    def _():
        pl.semaphore_wait(core_in, 1)
        greet_sibling()

    gelu(0)
    pl.when(c == 1)(x_begin)
    partial(1)
    z_group(0)
    pl.when(c == 0)(x_begin)
    z_group(1)
    partial(2)
    z_group(2)
    c_x.start()
    gelu(1)
    z_group(3)
    partial(3)
    z_group(4)
    gelu(2)
    x_second(0)
    z_group(5)
    x_third_local(0)
    z_group(6)
    gelu(3)
    z_group(7)
    x_third(0)
    z_group(8)
    split_w_in(0)
    z_group(9)
    split_w_in(1)
    z_group(10)
    split_w_in(2)
    z_group(11)
    split_w_in(3)
    z_group(12)
    y_first(0)
    z_group(13)
    split_inputs()
    z_group(14)
    y_second(0)
    z_group(15)
    hidden_sibling(0)
    x_first(1)
    z_group(16)
    y_third(0)
    z_group(17)
    z_group(18)
    hidden_sibling(1)
    hidden_sibling(2)
    z_group(19)
    x_second(1)
    z_group(20)
    y_first(1)
    y_second(1)
    x_third_local(1)
    y_own(0)
    y_final(0)
    x_third(1)
    y_third(1)
    y_own(1)
    x_own(0)
    x_final(0)
    hidden_sibling(3)
    x_own(1)
    v_final(0)
    y_final(1)
    x_final(1)
    v_final(1)

    def all_left(sends, first=0):
        for i in range(first, n_chunks):
            for send in sends:
                send(i).wait_send()

    pl.when(gx == 0)(lambda: all_left((right,), n_chunks - FLIGHT))
    pl.when((gx == 1) | (gx == 2))(lambda: all_left((right, left)))
    pl.when(gx == 3)(lambda: all_left((left,), n_chunks - FLIGHT))
    for copy in (*c_p, *c_g, c_x, *c_h):
        copy.wait_send()
    for m in range(6):
        for g in range(2):
            x_copy(g, m).wait_send()
        for t in range(PARTS):
            y_copy(t, m).wait_send()
    for t in range(PARTS):
        v_copy(t).wait_send()


def write_out(*refs):
    copies = [pltpu.make_async_copy(refs[n], refs[3 + n], refs[6].at[n]) for n in range(3)]
    for copy in copies:
        copy.start()
    for copy in copies:
        copy.wait()


def per_device(inputs, pre_act, w_in, w_out, grad_out):
    v = pltpu.VMEM
    dma = pltpu.SemaphoreType.DMA
    scratch = [
        v((TOK, WID), F32), v((2, TOK, HALF), F32), v((2 * TOK, WID), BF16), v((2 * TOK, WID), BF16),
        v((8, BLK, WID), F32), v((WID, WID), BF16), v((WID, WID), BF16),
        v((4, TOK, WID), F32), v((4, TOK, WID), BF16), v((4, TOK, WID), BF16),
        v((TOK, WID), F32), v((TOK, WID), F32), v((2 * TOK, WID), BF16), v((2 * TOK, WID), BF16),
        v((8, TOK, BLK), F32), v((4, TOK, BLK), F32), v((8, TOK, BLK), F32),
        v((4, BLK, 2 * TOK), BF16), v((4, BLK, 2 * TOK), BF16), v((4, BLK, 2 * TOK), BF16), v((4, BLK, 2 * TOK), BF16),
        *[v((8, TOK, BLK), F32)] * 5,
        v((TOK, WID), BF16), v((TOK, WID), BF16), v((4, TOK, BLK), F32), v((4, TOK, BLK), F32),
        v((2, 6, BLK, HALF), F32), v((2, 6, BLK, HALF), F32), v((2, 2, BLK, HALF), F32),
        v((PARTS, 6, ROWS // 2, 2 * BLK), F32), v((PARTS, 6, ROWS // 2, 2 * BLK), F32), v((PARTS, ROWS, 2 * BLK), F32),
        v((PARTS, ROWS, BLK), F32), v((PARTS, ROWS, BLK), F32),
        dma((22,)), dma((11,)), dma((11,)), dma((2, len(CHUNKS))), dma((2, len(CHUNKS))),
        dma((2, 6)), dma((2, 6)), dma((PARTS, 6)), dma((PARTS, 6)), dma((PARTS,)), dma((PARTS,)),
        *[pltpu.SemaphoreType.REGULAR] * 3,
    ]
    results = pl.pallas_call(
        kernel,
        out_shape=(v((TOK, BLK), F32), v((WID, BLK), F32), v((BLK, WID), F32)),
        in_specs=[pl.BlockSpec(memory_space=pl.ANY)] * 5,
        out_specs=[pl.BlockSpec(memory_space=pltpu.VMEM)] * 3,
        scratch_shapes=scratch,
        compiler_params=pltpu.CompilerParams(collective_id=0, has_side_effects=True, vmem_limit_bytes=60 << 20),
        cost_estimate=pl.CostEstimate(flops=6_442_450_944, bytes_accessed=13 << 20, transcendentals=1 << 19),
        name="mlp_backward",
    )(inputs, pre_act, w_in, w_out, grad_out)
    return pl.pallas_call(
        write_out,
        out_shape=[jax.ShapeDtypeStruct(r.shape, F32) for r in results],
        in_specs=[pl.BlockSpec(memory_space=pl.ANY)] * 3,
        out_specs=[pl.BlockSpec(memory_space=pl.ANY)] * 3,
        scratch_shapes=[dma((3,))],
        compiler_params=pltpu.CompilerParams(vmem_limit_bytes=2 << 20),
        name="write_out",
    )(*results)


def solution(mesh):
    in_specs = (P("gz", "gx"), P("gz", "gy"), P("gx", "gy"), P("gy", "gx"), P("gz", "gx"))
    out_specs = (P("gz", ("gx", "gy")), P("gx", ("gy", "gz")), P(("gy", "gz"), "gx"))
    return jax.shard_map(
        per_device, mesh=mesh, in_specs=in_specs, out_specs=out_specs, check_vma=False
    )
```
